32 devices in a mesh: dp: 8 (over z, x), mp: 4 (over y, core).
Axes of the slice: x: 2, y: 2, z: 4, core: 2. Of those that a mesh axis runs over, the one named last changes fastest.
Arguments:
- layer_input: bfloat16 [16384, 768], P(('dp', 'mp')), may hold values from -6 to 6
- lengths: int32 [8, 8], P('dp'), may hold values from 1 to 1024, 2048 in all within a row
- key_mask: int32 [16384], P('dp'), may hold values 0 or 1
- input_gain: float32 [768], replicated, may hold values from 0.5 to 1.5
- input_bias: float32 [768], replicated, may hold values from -3 to 3
- qkv_weight: bfloat16 [768, 3, 768], P('dp', None, 'mp'), may hold values from -0.21875 to 0.21875
- mixed_gain: float32 [768], P('mp'), may hold values from 0.5 to 1.5
- mixed_bias: float32 [768], P('mp'), may hold values from -3 to 3
- out_weight: bfloat16 [768, 768], P('mp', 'dp'), may hold values from -0.21875 to 0.21875
- ffn_gain: float32 [768], replicated, may hold values from 0.5 to 1.5
- ffn_bias: float32 [768], replicated, may hold values from -3 to 3
- fc1_weight: bfloat16 [768, 3072], P('dp', 'mp'), may hold values from -0.21875 to 0.21875
- fc1_bias: float32 [3072], P('mp'), may hold values from -3 to 3
- hidden_gain: float32 [3072], P('mp'), may hold values from 0.5 to 1.5
- hidden_bias: float32 [3072], P('mp'), may hold values from -3 to 3
- fc2_weight: bfloat16 [3072, 768], P('mp', 'dp'), may hold values from -0.109375 to 0.109375
- out_grad: bfloat16 [16384, 768], P(('dp', 'mp')), may hold values from -6 to 6
Outputs:
- layer_output: bfloat16 [16384, 768], P(('dp', 'mp'))
- input_grad: float32 [16384, 768], P(('dp', 'mp'))
- input_gain_grad: float32 [768], replicated
- input_bias_grad: float32 [768], replicated
- qkv_grad: float32 [768, 3, 768], P('dp', None, 'mp')
- mixed_gain_grad: float32 [768], replicated
- mixed_bias_grad: float32 [768], replicated
- out_weight_grad: float32 [768, 768], P('mp', 'dp')
- ffn_gain_grad: float32 [768], replicated
- ffn_bias_grad: float32 [768], replicated
- fc1_grad: float32 [768, 3072], P('dp', 'mp')
- fc1_bias_grad: float32 [3072], replicated
- hidden_gain_grad: float32 [3072], replicated
- hidden_bias_grad: float32 [3072], replicated
- fc2_grad: float32 [3072, 768], P('mp', 'dp')
The draws below stay inside these ranges and needn't reach their ends.
Inputs may be any that keep to these rules, and one draw needn't show every extreme that they name: Each row holds the lengths of 8 sequences packed in order into one group; a row sums to 2048 and its largest entry is exactly 1024.
All inputs are finite; a program needn't handle non-finite values. No bound on the sum of `key_mask` on one device may be relied on, other than what follows from the above.
Results may differ from the reference program's by a relative error of at most 0.012.
Values may be sent and summed in bfloat16 or wider, within the bound.
No kernel may reach another device: no remote copies, remote signals or barrier semaphores. Data moves between devices by JAX's collectives and lax.ppermute only.
A program may use at most 128 MiB of HBM per device.

```python
import math
import jax
import jax.numpy as jnp
import numpy as np
from jax import lax

D = 768
HEADS = 12
HEAD_DIM = 64
FF = 3072
TOK_DEV = 2048
SEQS = 8
MAXLEN = 1024
GROUPS = 8
TOKENS = 16384


def with_ends(array, key, least, top_value):
    spot = [jax.random.randint(jax.random.fold_in(key, axis), (), 0, length) for axis, length in enumerate(array.shape)]
    main_axis = array.shape.index(max(array.shape))
    neighbour = spot[:main_axis] + [(spot[main_axis] + 1) % array.shape[main_axis]] + spot[main_axis + 1:]
    return array.at[tuple(spot)].set(least).at[tuple(neighbour)].set(top_value)


def raised(drawn, stream_key, source, target, parts, factor):
    owner, partner = [(jnp.arange(drawn.shape[dim]) // (drawn.shape[dim] // parts)).reshape([-1 if axis == dim else 1 for axis in range(drawn.ndim)]) for dim in (source, target)]
    chosen = jax.random.permutation(stream_key, parts)[partner]
    strong = (owner == chosen) | (owner == (partner + parts // 2) % parts)
    return jnp.where(strong, factor * drawn, drawn)


def levels(rng, shape, shards, least, high):
    loudness = 1.0
    for axis_at, shards_of in shards:
        heights = jax.random.uniform(jax.random.fold_in(jax.random.fold_in(rng, 6), axis_at), (shards_of,), jnp.float32, least / len(shards), high / len(shards))
        loudness = loudness * jnp.repeat(jnp.exp(heights), shape[axis_at] // shards_of).reshape((-1,) + (1,) * (len(shape) - 1 - axis_at))
    return loudness


def split_up(number_of, total, limit, lean):
    portions = [(1 << 20) // math.isqrt(standing ** lean) + 1 for standing in range(2, number_of + 1)]
    spare, counts = total - limit - (number_of - 1), [1] * (number_of - 1)
    while spare > 0:
        movable = [i for i in range(number_of - 1) if counts[i] < limit]
        whole, remaining = sum([portions[i] for i in movable]), spare
        for i in movable:
            more = min(limit - counts[i], max(1, remaining * portions[i] // whole), spare)
            counts[i] = counts[i] + more
            spare = spare - more
    return np.array([limit] + counts)


def uneven_parts(key, number_of, total, limit, lean):
    if number_of == 2:
        one = jax.random.randint(key, (), max(1, total - limit), min(limit, total - 1) + 1)
        return jnp.stack([one, total - one])
    tallies = jnp.asarray(split_up(number_of, total, limit, lean), jnp.int32)
    twos = (number_of - 1) // 2
    source_of, sink = tallies[1:1 + 2 * twos:2], tallies[2:2 + 2 * twos:2]
    room = jnp.minimum(source_of - 1, limit - sink)
    passed = jax.random.randint(jax.random.fold_in(key, 1), (twos,), 0, 1 << 20) % (room + 1)
    tallies = tallies.at[1:1 + 2 * twos:2].set(source_of - passed).at[2:2 + 2 * twos:2].set(sink + passed)
    return tallies[jax.random.permutation(jax.random.fold_in(key, 2), number_of)]


def normal_values(key, shape, deviation, reach, split=(), kind=jnp.bfloat16):
    values = deviation * jax.random.normal(key, shape, jnp.float32)
    if split:
        values = values * levels(key, shape, split, -0.22, 0.18)
    return jnp.clip(values, -reach, reach).astype(kind)


def heavy_noise(stream_key, extent, width, reach, split, heavy, kind=jnp.bfloat16):
    values = width * jax.random.normal(stream_key, extent, jnp.float32)
    if split:
        values = values * levels(stream_key, extent, split, -0.22, 0.18)
    return jnp.clip(raised(values, jax.random.fold_in(stream_key, 3), *heavy), -reach, reach).astype(kind)


def setup_inputs(seed: int = 0) -> dict:
    streams_of = jax.random.split(jax.random.key(seed), 18)
    return {
        "layer_input": heavy_noise(streams_of[0], (TOKENS, D), 1.0, 6.0, ((0, 32),), (0, 1, 32, 2.75)),
        "lengths": jax.vmap(lambda own: uneven_parts(own, SEQS, TOK_DEV, MAXLEN, 2))(jax.random.split(streams_of[1], GROUPS)).reshape((GROUPS, SEQS)).astype(jnp.int32),
        "key_mask": with_ends((jax.random.randint(streams_of[2], (TOKENS,), 0, 8) < 7).astype(jnp.int32), jax.random.fold_in(streams_of[2], 1), 0, 1),
        "input_gain": jnp.clip(1.0 + 0.1 * jax.random.normal(streams_of[3], (D,), jnp.float32), 0.5, 1.5),
        "input_bias": normal_values(streams_of[4], (D,), 0.5, 3.0, (), jnp.float32),
        "qkv_weight": normal_values(streams_of[5], (D, 3, D), D ** -0.5, 0.21875, ((0, 8), (2, 4))),
        "mixed_gain": jnp.clip(1.0 + 0.1 * jax.random.normal(streams_of[6], (D,), jnp.float32), 0.5, 1.5),
        "mixed_bias": normal_values(streams_of[7], (D,), 0.5, 3.0, ((0, 4),), jnp.float32),
        "out_weight": normal_values(streams_of[8], (D, D), D ** -0.5, 0.21875, ((0, 4), (1, 8))),
        "ffn_gain": jnp.clip(1.0 + 0.1 * jax.random.normal(streams_of[9], (D,), jnp.float32), 0.5, 1.5),
        "ffn_bias": normal_values(streams_of[10], (D,), 0.5, 3.0, (), jnp.float32),
        "fc1_weight": normal_values(streams_of[11], (D, FF), D ** -0.5, 0.21875, ((0, 8), (1, 4))),
        "fc1_bias": normal_values(streams_of[12], (FF,), 0.5, 3.0, ((0, 4),), jnp.float32),
        "hidden_gain": jnp.clip(1.0 + 0.1 * jax.random.normal(streams_of[13], (FF,), jnp.float32), 0.5, 1.5),
        "hidden_bias": normal_values(streams_of[14], (FF,), 0.5, 3.0, ((0, 4),), jnp.float32),
        "fc2_weight": normal_values(streams_of[15], (FF, D), FF ** -0.5, 0.109375, ((0, 4), (1, 8))),
        "out_grad": heavy_noise(streams_of[16], (TOKENS, D), 1.0, 6.0, ((0, 32),), (0, 1, 32, 2.75)),
    }


EPS = 1e-05
HIGH = lax.Precision.HIGHEST

@jax.custom_vjp
def low(v):
    return lax.optimization_barrier(v.astype(jnp.bfloat16)).astype(jnp.float32)

@jax.custom_vjp
def low_back(v):
    return v

def low_keep(v):
    return (low(v), None)

def low_pass(kept, grad):
    return (grad,)

def back_keep(v):
    return (v, None)

def back_low(kept, grad):
    return (low(grad),)
low.defvjp(low_keep, low_pass)
low_back.defvjp(back_keep, back_low)

def layer_norm(values, norm_gain, norm_bias):
    row_mean = lax.optimization_barrier(jnp.mean(values, axis=-1, keepdims=True))
    centred = values - row_mean
    row_var = lax.optimization_barrier(jnp.mean(centred * centred, axis=-1, keepdims=True))
    return centred * lax.rsqrt(row_var + EPS) * norm_gain + norm_bias

def segment_ids(length_row, length_all):
    seq_ends = jnp.cumsum(length_row).astype(jnp.int32)
    places = jnp.arange(length_all, dtype=jnp.int32)
    return lax.optimization_barrier(jnp.sum((places[:, None] >= seq_ends[None, :]).astype(jnp.int32), axis=1)).astype(jnp.int32)

def attend_group(queries, key_mat, value_mat, segment, key_keep):
    length_all = queries.shape[0]
    block_rows = min(512, length_all)
    blocks = length_all // block_rows
    score_scale = HEAD_DIM ** (-0.5)
    columns = jnp.arange(length_all, dtype=jnp.int32)

    def one_block(inputs):
        block_q, first_row = inputs
        row_ids = first_row + jnp.arange(block_rows, dtype=jnp.int32)
        seg_rows = lax.dynamic_slice_in_dim(segment, first_row, block_rows, 0)
        allowed = (seg_rows[:, None] == segment[None, :]) & ((key_keep[None, :] == 1) | (row_ids[:, None] == columns[None, :]))
        scores = low_back(jnp.einsum('qhe,khe->hqk', block_q, key_mat, precision=HIGH) * score_scale)
        scores = jnp.where(allowed[None], scores, -1e+30)
        row_max = lax.optimization_barrier(jnp.max(scores, axis=-1, keepdims=True))
        exp_scores = jnp.exp(scores - row_max)
        probabilities = low(exp_scores / lax.optimization_barrier(jnp.sum(exp_scores, axis=-1, keepdims=True)))
        return jnp.einsum('hqk,khe->qhe', probabilities, value_mat, precision=HIGH)
    starts = jnp.arange(blocks, dtype=jnp.int32) * block_rows
    shaped = queries.reshape(blocks, block_rows, queries.shape[1], queries.shape[2])
    result = lax.map(jax.checkpoint(one_block), (shaped, starts))
    return result.reshape(queries.shape)

def reference(layer_input, lengths, key_mask, input_gain, input_bias, qkv_weight, mixed_gain, mixed_bias, out_weight, ffn_gain, ffn_bias, fc1_weight, fc1_bias, hidden_gain, hidden_bias, fc2_weight, out_grad):
    segment = jax.vmap(segment_ids, in_axes=(0, None))(lengths, TOK_DEV)
    key_keep = key_mask.reshape(GROUPS, TOK_DEV)
    floats = tuple((arr.astype(jnp.float32) for arr in (layer_input, input_gain, input_bias, qkv_weight, mixed_gain, mixed_bias, out_weight, ffn_gain, ffn_bias, fc1_weight, fc1_bias, hidden_gain, hidden_bias, fc2_weight)))

    def group_attend(inputs):
        return attend_group(*inputs)

    def forward(input_f, gain_in, bias_in, weight_qkv, gain_mix, bias_mix, weight_out, gain_ffn, bias_ffn, weight_one, bias_one, gain_hid, bias_hid, weight_two):
        lowered_in = low(layer_norm(input_f, gain_in, bias_in))
        projected = low(low_back(jnp.einsum('td,dcf->tcf', lowered_in, weight_qkv, precision=HIGH)))
        shaped = projected.reshape(GROUPS, TOK_DEV, 3, HEADS, HEAD_DIM)
        attended = lax.map(jax.checkpoint(group_attend), (shaped[:, :, 0], shaped[:, :, 1], shaped[:, :, 2], segment, key_keep))
        attended = low_back(attended.reshape(TOKENS, D))
        lowered_mix = low(layer_norm(attended, gain_mix, bias_mix))
        residual = input_f + low_back(jnp.dot(lowered_mix, weight_out, precision=HIGH))
        lowered_ffn = low(layer_norm(residual, gain_ffn, bias_ffn))
        pre_act = low_back(jnp.dot(lowered_ffn, weight_one, precision=HIGH) + bias_one)
        activated = jax.nn.gelu(pre_act, approximate=False)
        lowered_hid = low(layer_norm(activated, gain_hid, bias_hid))
        return residual + low_back(jnp.dot(lowered_hid, weight_two, precision=HIGH))
    output_f, pullback = jax.vjp(forward, *floats)
    grads = pullback(out_grad.astype(jnp.float32))
    return (output_f.astype(jnp.bfloat16), grads[0], grads[1], grads[2], grads[3], grads[4], grads[5], grads[6], grads[7], grads[8], grads[9], grads[10], grads[11], grads[12], grads[13])
```

```python
import functools

import jax
import jax.numpy as jnp
from jax import lax
from jax.experimental import pallas as pl
from jax.experimental.pallas import tpu as pltpu
from jax.sharding import PartitionSpec as P

HD = 64
EPS = 1e-05
BIG = 1e30
NT = (((1,), (1,)), ((), ()))
NN = (((1,), (0,)), ((), ()))
TN = (((0,), (0,)), ((), ()))
bf16 = jnp.bfloat16
f32 = jnp.float32
VMEM_LIMIT = 56 * 2**20


def dot(a, b, dims=NN):
    return lax.dot_general(a, b, dims, preferred_element_type=f32)


def split3(x):
    high = x.astype(bf16).astype(f32)
    rest = x - high
    mid = rest.astype(bf16).astype(f32)
    return high, mid, rest - mid


def head_tile(ref, rows, col):
    at = col // 128 * 128
    width = min(128, ref.shape[-1] - at)
    x = ref[rows, at : at + width].astype(f32)
    if width < 128:
        x = jnp.concatenate([x, jnp.zeros((x.shape[0], 128 - width), f32)], axis=1)
    if col % 128:
        x = pltpu.roll(x, 64, 1)
    return x


def pack_heads(parts, low):
    tiles = []
    for i in range(0, len(parts), 2):
        if i + 1 < len(parts):
            tiles.append(jnp.where(low, parts[i], pltpu.roll(parts[i + 1], 64, 1)))
        else:
            tiles.append(parts[i][:, :64])
    return tiles


def seq_ends(len_ref, nseq):
    ends, total = [], jnp.int32(0)
    for j in range(nseq):
        total = total + len_ref[0, j]
        ends.append(total)
    return ends


def key_range(ends, first, last):
    lo, hi, start = jnp.int32(0), jnp.int32(0), jnp.int32(0)
    for end in ends:
        lo = jnp.where(first >= end, end, lo)
        hi = jnp.where(last >= start, end, hi)
        start = end
    return lo, hi


def fwd_kernel(m_ref, len_ref, mask_ref, qa_in, qb_in, o_ref, of_ref, qa, ka, va, *, heads, chunk, BQ, BK, nseq):
    G = qa.shape[1]
    nch, W = G // chunk, heads * HD
    half = nch // 2
    m = m_ref[0]
    ends = seq_ends(len_ref, nseq)
    lane = lax.broadcasted_iota(jnp.int32, (1, 128), 1)
    startv = jnp.full((1, 128), 2**30, jnp.int32)
    endv = jnp.zeros((1, 128), jnp.int32)
    prev = jnp.int32(0)
    for j in range(nseq):
        startv = jnp.where(lane == 64 + j, prev, startv)
        endv = jnp.where(lane == 64 + j, ends[j], endv)
        prev = ends[j]
    lane_c = lax.broadcasted_iota(jnp.int32, (chunk, 128), 1)
    low = lane_c < 64
    segl = (lane_c >= 64) & (lane_c < 64 + nseq)
    ml = 64 + nseq
    for c in range(nch):
        lc = jnp.bitwise_xor(m, c)
        rows = slice(c * chunk, (c + 1) * chunk)
        src = qa_in if c < half else qb_in
        srows = slice(c % half * chunk, (c % half + 1) * chunk)
        rid = lc * chunk + lax.broadcasted_iota(jnp.int32, (chunk, 128), 0)
        keep = jnp.broadcast_to(mask_ref[pl.ds(lc, 1), :].astype(f32), (128, chunk)).T
        onehot = (rid >= startv) & (rid < endv)
        qfeat = jnp.where(segl, jnp.where(onehot, 1.0, 0.0), jnp.where(lane_c == ml, 1.0, 0.0))
        kfeat = jnp.where(
            segl,
            jnp.where(onehot, 0.0, -BIG),
            jnp.where(
                lane_c == ml,
                jnp.where(keep > 0.5, 0.0, -BIG),
                jnp.where((lane_c > ml) & (lane_c < ml + 4), 1.0, 0.0),
            ),
        )
        vfeat = jnp.where((lane_c >= 64) & (lane_c < 67), 1.0, 0.0)
        for h in range(heads):
            q = head_tile(src, srows, h * HD) * 0.125
            k = head_tile(src, srows, W + h * HD)
            v = head_tile(src, srows, 2 * W + h * HD)
            qa[h, rows, :] = jnp.where(low, q, qfeat).astype(bf16)
            ka[h, rows, :] = jnp.where(low, k, kfeat).astype(bf16)
            va[h, rows, :] = jnp.where(low, v, vfeat).astype(bf16)
    per, perk = chunk // BQ, chunk // BK
    lane_q = lax.broadcasted_iota(jnp.int32, (BQ, 128), 1)

    def qblock(b, _):
        off = pl.multiple_of(jnp.bitwise_xor(b // per, m) * chunk + (b % per) * BQ, BQ)
        rows = pl.ds(off, BQ)
        lo, hi = key_range(ends, b * BQ, b * BQ + BQ - 1)
        qs = [qa[h, rows, :] for h in range(heads)]
        init = []
        for h in range(heads):
            kk, vv = ka[h, rows, :].astype(f32), va[h, rows, :].astype(f32)
            own = jnp.sum(jnp.where(lane_q < 64, qs[h].astype(f32) * kk, 0.0), axis=1, keepdims=True)
            drop = jnp.sum(jnp.where(lane_q == ml, kk, 0.0), axis=1, keepdims=True) < -1.0
            init += [jnp.where(drop, own, -BIG), jnp.where(drop, vv, 0.0)]

        def kstep(kb, carry):
            koff = pl.multiple_of(jnp.bitwise_xor(kb // perk, m) * chunk + (kb % perk) * BK, BK)
            kr = pl.ds(koff, BK)
            out = []
            scores = [dot(qs[h], ka[h, kr, :], NT) for h in range(heads)]
            for h in range(heads):
                mx, acc = carry[2 * h], carry[2 * h + 1]
                new = jnp.maximum(mx, jnp.max(scores[h], axis=1, keepdims=True))
                p = jnp.exp(scores[h] - new).astype(bf16)
                out += [new, acc * jnp.exp(mx - new) + dot(p, va[h, kr, :])]
            return tuple(out)

        fin = lax.fori_loop(lo // BK, (hi + BK - 1) // BK, kstep, tuple(init))
        outs = []
        for h in range(heads):
            mx, acc = fin[2 * h], fin[2 * h + 1]
            total = acc[:, 64:65]
            outs.append(acc * (1.0 / total))
            l1, l2, l3 = split3(mx + jnp.log(total))
            feat = jnp.where(
                lane_q == ml + 1,
                -l1,
                jnp.where(lane_q == ml + 2, -l2, jnp.where(lane_q == ml + 3, -l3, qs[h].astype(f32))),
            )
            qa[h, rows, :] = feat.astype(bf16)
        full = jnp.concatenate(pack_heads(outs, lane_q < 64), axis=1)
        of_ref[rows, :] = full
        o_ref[rows, :] = full.astype(bf16)
        return 0

    lax.fori_loop(0, G // BQ, qblock, 0)


SMEM_SPEC = pl.BlockSpec(memory_space=pltpu.SMEM)
VMEM_SPEC = pl.BlockSpec(memory_space=pltpu.VMEM)


def attend_forward(m, lengths, mask, qkv_a, qkv_b, heads, chunk):
    G = 2 * qkv_a.shape[0]
    sh = jax.ShapeDtypeStruct
    return pl.pallas_call(
        functools.partial(fwd_kernel, heads=heads, chunk=chunk, BQ=256, BK=512, nseq=lengths.shape[1]),
        out_shape=(sh((G, heads * HD), bf16), sh((G, heads * HD), f32)) + (sh((heads, G, 128), bf16),) * 3,
        in_specs=[SMEM_SPEC, SMEM_SPEC, VMEM_SPEC, VMEM_SPEC, VMEM_SPEC],
        out_specs=[VMEM_SPEC] * 5,
        compiler_params=pltpu.CompilerParams(vmem_limit_bytes=VMEM_LIMIT),
        cost_estimate=pl.CostEstimate(flops=6 * 10**9, bytes_accessed=12 * 10**6, transcendentals=6 * 10**6),
        name="attend_forward",
    )(m, lengths, mask.reshape(G // chunk, chunk), qkv_a, qkv_b)


def bwd_kernel(m_ref, len_ref, qa, ka, va, of_ref, d0, d1, d2, d3, out_ref, doa, dqs, dka, dva, *, heads, chunk, BQ, BK, nseq):
    G = qa.shape[1]
    m = m_ref[0]
    ml = 64 + nseq
    ends = seq_ends(len_ref, nseq)
    lane_c = lax.broadcasted_iota(jnp.int32, (chunk, 128), 1)
    low = lane_c < 64
    for c, d in enumerate((d0, d1, d2, d3)):
        rows = slice(c * chunk, (c + 1) * chunk)
        for h in range(heads):
            do = jnp.where(low, head_tile(d, slice(None), h * HD), 0.0)
            o = head_tile(of_ref, rows, h * HD)
            row_dot = jnp.sum(jnp.where(low, do * o, 0.0), axis=1, keepdims=True)
            r1, r2, r3 = split3(row_dot)
            doa[h, rows, :] = jnp.where(
                lane_c == 64, -r1, jnp.where(lane_c == 65, -r2, jnp.where(lane_c == 66, -r3, do))
            ).astype(bf16)
            q, k, v = (ref[h, rows, :].astype(f32) for ref in (qa, ka, va))
            drop = jnp.sum(jnp.where(lane_c == ml, k, 0.0), axis=1, keepdims=True) < -1.0
            own = jnp.sum(jnp.where(low | (lane_c > ml), q * k, 0.0), axis=1, keepdims=True)
            p_own = jnp.where(drop, jnp.exp(jnp.where(drop, own, 0.0)), 0.0)
            ds_own = p_own * (jnp.sum(jnp.where(low, do * v, 0.0), axis=1, keepdims=True) - row_dot)
            dqs[h, rows, :] = ds_own * k
            dka[h, rows, :] = ds_own * q
            dva[h, rows, :] = p_own * do
    per, perk = chunk // BQ, chunk // BK

    def qblock(b, _):
        off = pl.multiple_of(jnp.bitwise_xor(b // per, m) * chunk + (b % per) * BQ, BQ)
        rows = pl.ds(off, BQ)
        lo, hi = key_range(ends, b * BQ, b * BQ + BQ - 1)

        def kstep(kb, carry):
            koff = pl.multiple_of(jnp.bitwise_xor(kb // perk, m) * chunk + (kb % perk) * BK, BK)
            kr = pl.ds(koff, BK)
            out = []
            scores = [dot(ka[h, kr, :], qa[h, rows, :], NT) for h in range(heads)]
            dps = [dot(va[h, kr, :], doa[h, rows, :], NT) for h in range(heads)]
            for h in range(heads):
                p = jnp.exp(scores[h])
                ds = (p * dps[h]).astype(bf16)
                dva[h, kr, :] += dot(p.astype(bf16), doa[h, rows, :])
                dka[h, kr, :] += dot(ds, qa[h, rows, :])
                out.append(carry[h] + dot(ds, ka[h, kr, :], TN))
            return tuple(out)

        zeros = tuple(jnp.zeros((BQ, 128), f32) for _ in range(heads))
        fin = lax.fori_loop(lo // BK, (hi + BK - 1) // BK, kstep, zeros)
        for h in range(heads):
            dqs[h, rows, :] += fin[h]
        return 0

    lax.fori_loop(0, G // BQ, qblock, 0)
    for c in range(G // chunk):
        rows = slice(c * chunk, (c + 1) * chunk)
        parts = [dqs[h, rows, :] * 0.125 for h in range(heads)]
        parts += [dka[h, rows, :] for h in range(heads)] + [dva[h, rows, :] for h in range(heads)]
        for i, tile in enumerate(pack_heads(parts, low)):
            out_ref[rows, 128 * i : 128 * i + tile.shape[1]] = tile.astype(bf16)


def attend_backward(m, lengths, qa, ka, va, of, grads, heads, chunk):
    G = qa.shape[1]
    return pl.pallas_call(
        functools.partial(bwd_kernel, heads=heads, chunk=chunk, BQ=256, BK=256, nseq=lengths.shape[1]),
        out_shape=jax.ShapeDtypeStruct((G, 3 * heads * HD), bf16),
        in_specs=[SMEM_SPEC, SMEM_SPEC] + [VMEM_SPEC] * 8,
        out_specs=VMEM_SPEC,
        scratch_shapes=[pltpu.VMEM((heads, G, 128), bf16)] + [pltpu.VMEM((heads, G, 128), f32)] * 3,
        compiler_params=pltpu.CompilerParams(vmem_limit_bytes=VMEM_LIMIT),
        cost_estimate=pl.CostEstimate(flops=15 * 10**9, bytes_accessed=12 * 10**6, transcendentals=6 * 10**6),
        name="attend_backward",
    )(m, lengths, qa, ka, va, of, *grads)


def gelu_parts(u):
    z = jnp.abs(u) * 0.7071067811865476
    t = 1.0 / (1.0 + 0.3275911 * z)
    poly = t * (0.254829592 + t * (-0.284496736 + t * (1.421413741 + t * (-1.453152027 + t * 1.061405429))))
    e = jnp.exp(-z * z)
    tail = 0.5 * poly * e
    cdf = jnp.where(u >= 0, 1.0 - tail, tail)
    return u * cdf, cdf + u * (e * 0.3989422804014327)


def ffn_in_kernel(x_ref, w_ref, b_ref, g_ref, og_ref, v_ref, a_ref, gp_ref, e_ref, st_ref):
    u = dot(x_ref[...], w_ref[...]) + b_ref[...]
    a, gp = gelu_parts(u)
    e = dot(og_ref[...], v_ref[...])
    n = a.shape[1]
    mean = jnp.sum(a, axis=1, keepdims=True) * (1.0 / n)
    cent = a - mean
    m2 = jnp.sum(cent * cent, axis=1, keepdims=True)
    eg = e * g_ref[...]
    t1 = jnp.sum(eg, axis=1, keepdims=True)
    t2 = jnp.sum(eg * cent, axis=1, keepdims=True)
    a_ref[...] = a.astype(a_ref.dtype)
    gp_ref[...] = gp.astype(gp_ref.dtype)
    e_ref[...] = e.astype(e_ref.dtype)
    lane = lax.broadcasted_iota(jnp.int32, (a.shape[0], 128), 1)
    st = jnp.where(lane == 0, mean, jnp.where(lane == 1, m2, jnp.where(lane == 2, t1, t2)))
    st_ref[...] = st.T[:8]


def ffn_in(x, w, b, g, og, v, rows=256):
    R, D = x.shape
    F = w.shape[1]
    full = lambda i: (0, 0)
    row = lambda i: (i, 0)
    sh = jax.ShapeDtypeStruct
    return pl.pallas_call(
        ffn_in_kernel,
        grid=(R // rows,),
        in_specs=[
            pl.BlockSpec((rows, D), row),
            pl.BlockSpec((D, F), full),
            pl.BlockSpec((1, F), full),
            pl.BlockSpec((1, F), full),
            pl.BlockSpec((rows, D), row),
            pl.BlockSpec((D, F), full),
        ],
        out_specs=[pl.BlockSpec((rows, F), row)] * 3 + [pl.BlockSpec((8, rows), lambda i: (0, i))],
        out_shape=[sh((R, F), f32), sh((R, F), bf16), sh((R, F), f32), sh((8, R), f32)],
        compiler_params=pltpu.CompilerParams(vmem_limit_bytes=VMEM_LIMIT),
        cost_estimate=pl.CostEstimate(flops=4 * R * D * F, bytes_accessed=16 * R * F, transcendentals=2 * R * F),
        name="ffn_in",
    )(x, w, b, g, og, v)


def ffn_back_kernel(a_ref, gp_ref, e_ref, s0, s1, s2, s3, g_ref, b_ref, w_ref, fl_ref, du_ref, dx_ref, acc_ref, *, full_width):
    stats = [s[...] for s in (s0, s1, s2, s3)]
    n = a_ref.shape[1]
    means = [s[0:1] for s in stats]
    mean = sum(means) / len(stats)
    m2 = sum(s[1:2] + n * (mu - mean) * (mu - mean) for s, mu in zip(stats, means))
    inv = lax.rsqrt(m2 / full_width + EPS)
    c1 = sum(s[2:3] for s in stats) / full_width
    c2 = inv * sum(s[3:4] + (mu - mean) * s[2:3] for s, mu in zip(stats, means)) / full_width
    sub = lax.broadcasted_iota(jnp.int32, (128, mean.shape[1]), 0)
    cols = jnp.where(sub == 0, mean, jnp.where(sub == 1, inv, jnp.where(sub == 2, c1, c2))).T
    mean, inv, c1, c2 = (cols[:, i : i + 1] for i in range(4))
    e = e_ref[...].astype(f32)
    u = (a_ref[...].astype(f32) - mean) * inv
    fl_ref[...] = (u * g_ref[...] + b_ref[...]).astype(bf16)
    du = (gp_ref[...].astype(f32) * (inv * (e * g_ref[...] - c1 - u * c2))).astype(bf16)
    du_ref[...] = du
    dx_ref[...] = dot(du, w_ref[...], NT).astype(dx_ref.dtype)

    @pl.when(pl.program_id(0) == 0)
    def _():
        acc_ref[...] = jnp.zeros_like(acc_ref)

    acc_ref[0:1, :] += jnp.sum(e * u, axis=0, keepdims=True)
    acc_ref[1:2, :] += jnp.sum(e, axis=0, keepdims=True)
    acc_ref[2:3, :] += jnp.sum(du.astype(f32), axis=0, keepdims=True)


def ffn_back(a, gp, e, stats, g, b, w, full_width, rows=256):
    R, F = a.shape
    D = w.shape[0]
    full = lambda i: (0, 0)
    row = lambda i: (i, 0)
    sh = jax.ShapeDtypeStruct
    return pl.pallas_call(
        functools.partial(ffn_back_kernel, full_width=full_width),
        grid=(R // rows,),
        in_specs=[pl.BlockSpec((rows, F), row)] * 3
        + [pl.BlockSpec((8, rows), lambda i: (0, i))] * 4
        + [pl.BlockSpec((1, F), full), pl.BlockSpec((1, F), full), pl.BlockSpec((D, F), full)],
        out_specs=[pl.BlockSpec((rows, F), row)] * 2 + [pl.BlockSpec((rows, D), row), pl.BlockSpec((8, F), full)],
        out_shape=[sh((R, F), bf16), sh((R, F), bf16), sh((R, D), bf16), sh((8, F), f32)],
        compiler_params=pltpu.CompilerParams(vmem_limit_bytes=VMEM_LIMIT),
        cost_estimate=pl.CostEstimate(flops=2 * R * D * F, bytes_accessed=16 * R * F, transcendentals=0),
        name="ffn_back",
    )(a, gp, e, *stats, g, b, w)


def norm(values, gain, bias):
    mean = jnp.mean(values, axis=-1, keepdims=True)
    cent = values - mean
    inv = lax.rsqrt(jnp.mean(cent * cent, axis=-1, keepdims=True) + EPS)
    unit = cent * inv
    return unit * gain + bias, unit, inv


def norm_back(grad, unit, inv, gain):
    scaled = grad * gain
    first = jnp.mean(scaled, axis=-1, keepdims=True)
    second = jnp.mean(scaled * unit, axis=-1, keepdims=True)
    return inv * (scaled - first - unit * second), jnp.sum(grad * unit, axis=0), jnp.sum(grad, axis=0)


def swap(x, axis, k):
    n = lax.axis_size(axis)
    return lax.ppermute(x, axis, [(i, i ^ k) for i in range(n)])


def shift(x, axis, k):
    n = lax.axis_size(axis)
    return lax.ppermute(x, axis, [(i, (i + k) % n) for i in range(n)])


def gather_rows(x):
    x2 = swap(x, "mp", 2)
    return [x, swap(x, "mp", 1), x2, swap(x2, "mp", 1)]


def gather_weight(w):
    n = lax.axis_size("dp")
    if n != 8:
        return lax.all_gather(w, "dp", axis=0, tiled=True)
    i = lax.axis_index("dp")
    pieces, here = [], w
    for hop in range(4):
        pieces.append((here, hop, 0))
        pieces.append((swap(here, "dp", 1), hop, 1))
        if hop < 3:
            here = shift(here, "dp", 2)
    full = jnp.zeros((n * w.shape[0], w.shape[1]), w.dtype)
    for piece, hop, k in pieces:
        owner = ((i - 2 * hop) % n) ^ k
        full = lax.dynamic_update_slice_in_dim(full, piece, owner * w.shape[0], 0)
    return full


def scatter_weight(g):
    n = lax.axis_size("dp")
    if n != 8:
        return lax.psum_scatter(g, "dp", scatter_dimension=0, tiled=True)
    i = lax.axis_index("dp")
    rows = g.shape[0] // n
    blocks = g.reshape(n // 2, 2, rows, g.shape[1])
    here = lax.dynamic_index_in_dim(blocks, i % 2, 1, keepdims=False)
    other = lax.dynamic_index_in_dim(blocks, 1 - i % 2, 1, keepdims=False)
    mine = here + swap(other.astype(bf16), "dp", 1).astype(f32)
    z = i // 2
    carry = lax.dynamic_index_in_dim(mine, (z + 3) % 4, 0, keepdims=False)
    for hop in range(1, 4):
        arrived = shift(carry.astype(bf16), "dp", 2).astype(f32)
        carry = arrived + lax.dynamic_index_in_dim(mine, (z + 3 - hop) % 4, 0, keepdims=False)
    return carry


def scatter_rows(far, near):
    f = far()
    r = f.shape[0] // 2
    pair = f[:r].astype(f32) + swap(f[r:].astype(bf16), "mp", 1).astype(f32)
    sent = swap(pair.astype(bf16), "mp", 2)
    n = near()
    own = n[:r].astype(f32) + swap(n[r:].astype(bf16), "mp", 1).astype(f32)
    return own + sent.astype(f32)


def per_device(
    layer_input,
    lengths,
    key_mask,
    input_gain,
    input_bias,
    qkv_weight,
    mixed_gain,
    mixed_bias,
    out_weight,
    ffn_gain,
    ffn_bias,
    fc1_weight,
    fc1_bias,
    hidden_gain,
    hidden_bias,
    fc2_weight,
    out_grad,
):
    R, D = layer_input.shape
    G = key_mask.shape[0]
    W = out_weight.shape[0]
    F = fc1_bias.shape[0]
    mp = lax.axis_size("mp")
    heads = W // HD
    m = lax.axis_index("mp").astype(jnp.int32)
    m1 = m.reshape(1)

    shard = qkv_weight.shape[0]
    qkv_out = jnp.concatenate([qkv_weight.reshape(shard, 3 * W), out_weight.T], axis=1)
    qkv_out = gather_weight(qkv_out)
    qkv_full, out_t = qkv_out[:, : 3 * W], qkv_out[:, 3 * W :]
    fc_full = lax.all_gather(jnp.concatenate([fc1_weight, fc2_weight.T], axis=1), "dp", axis=0, tiled=True)
    fc1_full, fc2_t = fc_full[:, :F], fc_full[:, F:]

    x = layer_input.astype(f32)
    normed, unit_in, inv_in = norm(x, input_gain, input_bias)
    xl = gather_rows(normed.astype(bf16))
    xl_a, xl_b = jnp.concatenate(xl[:2], axis=0), jnp.concatenate(xl[2:], axis=0)
    qkv_a = dot(xl_a, qkv_full).astype(bf16)
    qkv_b = dot(xl_b, qkv_full).astype(bf16)
    o, of, qa, ka, va = attend_forward(m1, lengths, key_mask, qkv_a, qkv_b, heads, R)
    attn = [o[:R]] + [swap(o[k * R : (k + 1) * R], "mp", k) for k in (1, 2, 3)]
    gains = jnp.stack([mixed_gain, mixed_bias])
    gains = gather_rows(gains)
    mixed_g = jnp.concatenate([v[0] for v in gains])
    mixed_b = jnp.concatenate([v[1] for v in gains])
    out_ts = gather_rows(out_t)
    outx = jnp.concatenate(out_ts, axis=1)
    ol, unit_mix, inv_mix = norm(jnp.concatenate(attn, axis=1).astype(f32), mixed_g, mixed_b)
    ol = ol.astype(bf16)
    h = x + dot(ol, outx, NT)
    hl, unit_ffn, inv_ffn = norm(h, ffn_gain, ffn_bias)
    hl = gather_rows(hl.astype(bf16))
    og = gather_rows(out_grad)
    hl_a, hl_b = jnp.concatenate(hl[:2], axis=0), jnp.concatenate(hl[2:], axis=0)
    og_a, og_b = jnp.concatenate(og[:2], axis=0), jnp.concatenate(og[2:], axis=0)
    b1, hg, hb = fc1_bias.reshape(1, F), hidden_gain.reshape(1, F), hidden_bias.reshape(1, F)
    in_a = ffn_in(hl_a, fc1_full, b1, hg, og_a, fc2_t)
    in_b = ffn_in(hl_b, fc1_full, b1, hg, og_b, fc2_t)
    st = jnp.concatenate([in_a[3], in_b[3]], axis=1)
    stats = [st]
    for k in (1, 2, 3):
        got = swap(st, "mp", k)
        stats.append(jnp.concatenate([got[:, (c ^ k) * R : ((c ^ k) + 1) * R] for c in range(mp)], axis=1))
    far_back = ffn_back(*in_b[:3], [s[:, 2 * R :] for s in stats], hg, hb, fc1_full, mp * F)
    near_back = ffn_back(*in_a[:3], [s[:, : 2 * R] for s in stats], hg, hb, fc1_full, mp * F)
    dhl = scatter_rows(lambda: far_back[2], lambda: near_back[2])
    fl_a, fl_b, du_a, du_b = near_back[0], far_back[0], near_back[1], far_back[1]
    hidden_sums = near_back[3] + far_back[3]
    fc2_t_grad = dot(og_a, fl_a, TN) + dot(og_b, fl_b, TN)
    fc1_grad = dot(hl_a, du_a, TN) + dot(hl_b, du_b, TN)
    fc_grad = jnp.concatenate([fc1_grad, fc2_t_grad], axis=1).astype(bf16)
    fc_grad = lax.psum_scatter(fc_grad, "dp", scatter_dimension=0, tiled=True).astype(f32)

    dh, ffn_gain_grad, ffn_bias_grad = norm_back(dhl, unit_ffn, inv_ffn, ffn_gain)
    dh = dh + out_grad.astype(f32)
    dhr = dh.astype(bf16)
    dol = dot(dhr, outx)
    datt, mixed_gain_grad, mixed_bias_grad = norm_back(dol, unit_mix, inv_mix, mixed_g)
    datt = datt.astype(bf16)
    pieces = [datt[:, :W]] + [swap(datt[:, k * W : (k + 1) * W], "mp", k) for k in (1, 2, 3)]
    dqkv = attend_backward(m1, lengths, qa, ka, va, of, pieces, heads, R)
    layer_output = h + scatter_rows(lambda: dot(fl_b, fc2_t, NT), lambda: dot(fl_a, fc2_t, NT))
    dqkv_a, dqkv_b = dqkv[: 2 * R], dqkv[2 * R :]
    dxl = scatter_rows(lambda: dot(dqkv_b, qkv_full, NT), lambda: dot(dqkv_a, qkv_full, NT))
    qkv_grad = dot(xl_a, dqkv_a, TN) + dot(xl_b, dqkv_b, TN)
    og_part = dot(ol, dhr, TN)
    out_grad_rows = scatter_rows(lambda: og_part[2 * W :], lambda: og_part[: 2 * W])
    both = scatter_weight(jnp.concatenate([qkv_grad, out_grad_rows.T], axis=1))
    din, input_gain_grad, input_bias_grad = norm_back(dxl, unit_in, inv_in, input_gain)
    input_grad = dh + din

    def placed(vector, k):
        width = mp * vector.shape[0]
        return lax.dynamic_update_slice_in_dim(
            jnp.zeros((width,), f32), vector, (m ^ k) * vector.shape[0], 0
        )

    def placed_xor(vector):
        return sum(placed(vector[k * W : (k + 1) * W], k) for k in range(mp))

    vectors = [
        input_gain_grad,
        input_bias_grad,
        placed_xor(mixed_gain_grad),
        placed_xor(mixed_bias_grad),
        ffn_gain_grad,
        ffn_bias_grad,
        placed(hidden_sums[2], 0),
        placed(hidden_sums[0], 0),
        placed(hidden_sums[1], 0),
    ]
    summed = lax.psum(jnp.concatenate(vectors), ("dp", "mp"))
    parts, at = [], 0
    for v in vectors:
        parts.append(summed[at : at + v.shape[0]])
        at += v.shape[0]
    return (
        layer_output.astype(bf16),
        input_grad,
        parts[0],
        parts[1],
        both[:, : 3 * W].reshape(shard, 3, W),
        parts[2],
        parts[3],
        both[:, 3 * W :].T,
        parts[4],
        parts[5],
        fc_grad[:, :F],
        parts[6],
        parts[7],
        parts[8],
        fc_grad[:, F:].T,
    )


def solution(mesh):
    return jax.shard_map(
        per_device,
        mesh=mesh,
        in_specs=(
            P(("dp", "mp"), None),
            P("dp", None),
            P("dp"),
            P(),
            P(),
            P("dp", None, "mp"),
            P("mp"),
            P("mp"),
            P("mp", "dp"),
            P(),
            P(),
            P("dp", "mp"),
            P("mp"),
            P("mp"),
            P("mp"),
            P("mp", "dp"),
            P(("dp", "mp"), None),
        ),
        out_specs=(
            P(("dp", "mp"), None),
            P(("dp", "mp"), None),
            P(),
            P(),
            P("dp", None, "mp"),
            P(),
            P(),
            P("mp", "dp"),
            P(),
            P(),
            P("dp", "mp"),
            P(),
            P(),
            P(),
            P("mp", "dp"),
        ),
        check_vma=False,
    )
```

```python
import functools

import jax
import jax.numpy as jnp
from jax import lax
from jax.experimental import pallas as pl
from jax.experimental.pallas import tpu as pltpu
from jax.sharding import PartitionSpec as P

HD = 64
EPS = 1e-05
BIG = 1e30
NT = (((1,), (1,)), ((), ()))
NN = (((1,), (0,)), ((), ()))
TN = (((0,), (0,)), ((), ()))
bf16 = jnp.bfloat16
f32 = jnp.float32


def dot(a, b, dims=NN):
    return lax.dot_general(a, b, dims, preferred_element_type=f32)


def split3(x):
    high = x.astype(bf16).astype(f32)
    rest = x - high
    mid = rest.astype(bf16).astype(f32)
    return high, mid, rest - mid


def head_tile(x, col):
    at = col // 128 * 128
    tile = x[:, at : at + 128].astype(f32)
    if tile.shape[1] < 128:
        tile = jnp.concatenate([tile, jnp.zeros((tile.shape[0], 128 - tile.shape[1]), f32)], axis=1)
    return pltpu.roll(tile, 64, 1) if col % 128 else tile


def pack_heads(parts, low):
    tiles = []
    for i in range(0, len(parts), 2):
        if i + 1 < len(parts):
            tiles.append(jnp.where(low, parts[i], pltpu.roll(parts[i + 1], 64, 1)))
        else:
            tiles.append(parts[i][:, :64])
    return tiles


def seq_ends(len_ref, nseq):
    ends, total = [], jnp.int32(0)
    for j in range(nseq):
        total = total + len_ref[0, j]
        ends.append(total)
    return ends


def key_range(ends, first, last):
    lo, hi, start = jnp.int32(0), jnp.int32(0), jnp.int32(0)
    for end in ends:
        lo = jnp.where(first >= end, end, lo)
        hi = jnp.where(last >= start, end, hi)
        start = end
    return lo, hi


def prepare(m, ends, mask_ref, xs, w_ref, qas, ka, va, heads, nseq):
    chunk = xs[0].shape[0]
    W = heads * HD
    lane = lax.broadcasted_iota(jnp.int32, (1, 128), 1)
    startv = jnp.full((1, 128), 2**30, jnp.int32)
    endv = jnp.zeros((1, 128), jnp.int32)
    prev = jnp.int32(0)
    for j in range(nseq):
        startv = jnp.where(lane == 64 + j, prev, startv)
        endv = jnp.where(lane == 64 + j, ends[j], endv)
        prev = ends[j]
    lane_c = lax.broadcasted_iota(jnp.int32, (chunk, 128), 1)
    low = lane_c < 64
    segl = (lane_c >= 64) & (lane_c < 64 + nseq)
    ml = 64 + nseq
    vfeat = jnp.where((lane_c >= 64) & (lane_c < 67), 1.0, 0.0)
    for c, x_ref in enumerate(xs):
        lc = jnp.bitwise_xor(m, c)
        rows = slice(c * chunk, (c + 1) * chunk)
        qkv = dot(x_ref[...], w_ref[...]).astype(bf16)
        rid = lc * chunk + lax.broadcasted_iota(jnp.int32, (chunk, 128), 0)
        keep = jnp.broadcast_to(mask_ref[pl.ds(lc, 1), :].astype(f32), (128, chunk)).T
        onehot = (rid >= startv) & (rid < endv)
        qfeat = jnp.where(segl, jnp.where(onehot, 1.0, 0.0), jnp.where(lane_c == ml, 1.0, 0.0))
        kfeat = jnp.where(
            segl,
            jnp.where(onehot, 0.0, -BIG),
            jnp.where(
                lane_c == ml,
                jnp.where(keep > 0.5, 0.0, -BIG),
                jnp.where((lane_c > ml) & (lane_c < ml + 4), 1.0, 0.0),
            ),
        )
        for h in range(heads):
            q = head_tile(qkv, h * HD) * 0.125
            k = head_tile(qkv, W + h * HD)
            v = head_tile(qkv, 2 * W + h * HD)
            qas[c // 2][h, c % 2 * chunk : (c % 2 + 1) * chunk, :] = jnp.where(low, q, qfeat).astype(bf16)
            ka[h, rows, :] = jnp.where(low, k, kfeat).astype(bf16)
            va[h, rows, :] = jnp.where(low, v, vfeat).astype(bf16)


def attend_rows(m, ends, part, qa, qout, ka, va, outs, of_ref, *, heads, chunk, BQ, BK, nseq):
    per, perk = chunk // BQ, chunk // BK
    ml = 64 + nseq
    lane_q = lax.broadcasted_iota(jnp.int32, (BQ, 128), 1)

    def qblock(b, out_ref, c):
        first = jnp.bitwise_xor(m, c) * chunk + b * BQ
        at = pl.multiple_of(b * BQ, BQ)
        own_rows = pl.ds(pl.multiple_of(c * chunk + b * BQ, BQ), BQ)
        rows = pl.ds(pl.multiple_of(c % 2 * chunk + b * BQ, BQ), BQ)
        lo, hi = key_range(ends, first, first + BQ - 1)
        qs = [qa[h, rows, :] for h in range(heads)]
        init = []
        for h in range(heads):
            kk, vv = ka[h, own_rows, :].astype(f32), va[h, own_rows, :].astype(f32)
            own = jnp.sum(jnp.where(lane_q < 64, qs[h].astype(f32) * kk, 0.0), axis=1, keepdims=True)
            drop = jnp.sum(jnp.where(lane_q == ml, kk, 0.0), axis=1, keepdims=True) < -1.0
            init += [jnp.where(drop, own, -BIG), jnp.where(drop, vv, 0.0)]

        def kstep(kb, carry):
            koff = pl.multiple_of(jnp.bitwise_xor(kb // perk, m) * chunk + (kb % perk) * BK, BK)
            kr = pl.ds(koff, BK)
            out = []
            scores = [dot(qs[h], ka[h, kr, :], NT) for h in range(heads)]
            for h in range(heads):
                mx, acc = carry[2 * h], carry[2 * h + 1]
                new = jnp.maximum(mx, jnp.max(scores[h], axis=1, keepdims=True))
                p = jnp.exp(scores[h] - new).astype(bf16)
                out += [new, acc * jnp.exp(mx - new) + dot(p, va[h, kr, :])]
            return tuple(out)

        fin = lax.fori_loop(lo // BK, (hi + BK - 1) // BK, kstep, tuple(init))
        heads_out = []
        for h in range(heads):
            mx, acc = fin[2 * h], fin[2 * h + 1]
            total = acc[:, 64:65]
            heads_out.append(acc * (1.0 / total))
            l1, l2, l3 = split3(mx + jnp.log(total))
            feat = jnp.where(
                lane_q == ml + 1,
                -l1,
                jnp.where(lane_q == ml + 2, -l2, jnp.where(lane_q == ml + 3, -l3, qs[h].astype(f32))),
            )
            qout[h, rows, :] = feat.astype(bf16)
        full = jnp.concatenate(pack_heads(heads_out, lane_q < 64), axis=1)
        of_ref[rows, :] = full
        out_ref[pl.ds(at, BQ), :] = full.astype(bf16)

    for c, out_ref in zip((2 * part, 2 * part + 1), outs):

        def step(b, _, c=c, out_ref=out_ref):
            qblock(b, out_ref, c)
            return 0

        lax.fori_loop(0, per, step, 0)


def fwd_far_kernel(m_ref, len_ref, mask_ref, x0, x1, x2, x3, w_ref, o2, o3, of_ref, q_far, q_near, ka, va, *, heads, BQ, BK, nseq):
    m = m_ref[0]
    ends = seq_ends(len_ref, nseq)
    prepare(m, ends, mask_ref, (x0, x1, x2, x3), w_ref, (q_near, q_far), ka, va, heads, nseq)
    attend_rows(m, ends, 1, q_far, q_far, ka, va, (o2, o3), of_ref, heads=heads, chunk=x0.shape[0], BQ=BQ, BK=BK, nseq=nseq)


def fwd_near_kernel(m_ref, len_ref, q_near, ka, va, o0, o1, of_ref, q_out, *, heads, BQ, BK, nseq):
    m = m_ref[0]
    ends = seq_ends(len_ref, nseq)
    attend_rows(m, ends, 0, q_near, q_out, ka, va, (o0, o1), of_ref, heads=heads, chunk=o0.shape[0], BQ=BQ, BK=BK, nseq=nseq)


SMEM_SPEC = pl.BlockSpec(memory_space=pltpu.SMEM)
VMEM_SPEC = pl.BlockSpec(memory_space=pltpu.VMEM)
ANY_SPEC = pl.BlockSpec(memory_space=pl.ANY)
AF_VMEM = pltpu.CompilerParams(vmem_limit_bytes=24 * 2**20)
AB_VMEM = pltpu.CompilerParams(vmem_limit_bytes=42 * 2**20)
BIG_VMEM = pltpu.CompilerParams(vmem_limit_bytes=56 * 2**20)
MID_VMEM = pltpu.CompilerParams(vmem_limit_bytes=34 * 2**20)
SMALL_VMEM = pltpu.CompilerParams(vmem_limit_bytes=20 * 2**20)
sds = jax.ShapeDtypeStruct


def whole(x):
    return pl.BlockSpec(x.shape, lambda i: (0,) * x.ndim)


def tie_kernel(*refs, n, others):
    for x, out in zip(refs[:n], refs[n + others :]):
        out[...] = x[...]


def tie(xs, *others):
    n = len(xs)
    return pl.pallas_call(
        functools.partial(tie_kernel, n=n, others=len(others)),
        out_shape=[sds(x.shape, x.dtype) for x in xs],
        in_specs=[VMEM_SPEC] * n + [ANY_SPEC] * len(others),
        out_specs=[VMEM_SPEC] * n,
        compiler_params=SMALL_VMEM,
        cost_estimate=cost(1, 1),
        name="tie",
    )(*xs, *others)


def add_kernel(*refs, n):
    refs[-1][...] = sum(x[...].astype(f32) for x in refs[:n]).astype(refs[-1].dtype)


def add(xs, *others):
    return pl.pallas_call(
        functools.partial(add_kernel, n=len(xs)),
        out_shape=sds(xs[0].shape, xs[0].dtype),
        in_specs=[VMEM_SPEC] * len(xs) + [ANY_SPEC] * len(others),
        out_specs=VMEM_SPEC,
        compiler_params=SMALL_VMEM,
        cost_estimate=cost(1, 1),
        name="add",
    )(*xs, *others)


def cost(flops, nbytes, trans=0):
    return pl.CostEstimate(flops=int(flops), bytes_accessed=int(nbytes), transcendentals=int(trans))


def attend_far(m, lengths, mask, xs, w, heads):
    chunk, G = xs[0].shape[0], mask.shape[0]
    W = heads * HD
    return pl.pallas_call(
        functools.partial(fwd_far_kernel, heads=heads, BQ=256, BK=512, nseq=lengths.shape[1]),
        out_shape=(sds((chunk, W), bf16),) * 2
        + (sds((G // 2, W), f32),)
        + (sds((heads, G // 2, 128), bf16),) * 2
        + (sds((heads, G, 128), bf16),) * 2,
        in_specs=[SMEM_SPEC, SMEM_SPEC] + [VMEM_SPEC] * 6,
        out_specs=[VMEM_SPEC] * 7,
        compiler_params=AF_VMEM,
        cost_estimate=cost(20e9, 12e6, 3e6),
        name="attend_far",
    )(m, lengths, mask.reshape(G // chunk, chunk), *xs, w)


def attend_near(m, lengths, q_near, ka, va):
    heads, half, _ = q_near.shape
    W = heads * HD
    return pl.pallas_call(
        functools.partial(fwd_near_kernel, heads=heads, BQ=256, BK=512, nseq=lengths.shape[1]),
        out_shape=(sds((half // 2, W), bf16),) * 2 + (sds((half, W), f32), sds(q_near.shape, bf16)),
        in_specs=[SMEM_SPEC, SMEM_SPEC] + [VMEM_SPEC] * 3,
        out_specs=[VMEM_SPEC] * 4,
        compiler_params=AF_VMEM,
        cost_estimate=cost(20e9, 12e6, 3e6),
        name="attend_near",
    )(m, lengths, q_near, ka, va)


def bwd_kernel(m_ref, len_ref, i_ref, qn, qf, ka, va, ofn, off, d0, d1, d2, d3, x0, x1, x2, x3, w_ref, dep, out_ref, far2_ref, far_ref, here_ref, other_ref, vec_ref, qa, doa, dqs, dka, dva, grad, sums, *, heads, chunk, BQ, BK, nseq, n):
    G = ka.shape[1]
    m = m_ref[0]
    ml = 64 + nseq
    ends = seq_ends(len_ref, nseq)
    lane_c = lax.broadcasted_iota(jnp.int32, (chunk, 128), 1)
    low = lane_c < 64
    for c, d in enumerate((d0, d1, d2, d3)):
        rows = slice(c * chunk, (c + 1) * chunk)
        pair = slice(c % 2 * chunk, (c % 2 + 1) * chunk)
        for h in range(heads):
            do = jnp.where(low, head_tile(d[:chunk, :], h * HD), 0.0)
            o = head_tile((ofn, off)[c // 2][pair, :], h * HD)
            qa[h, rows, :] = (qn, qf)[c // 2][h, pair, :]
            row_dot = jnp.sum(jnp.where(low, do * o, 0.0), axis=1, keepdims=True)
            r1, r2, r3 = split3(row_dot)
            doa[h, rows, :] = jnp.where(
                lane_c == 64, -r1, jnp.where(lane_c == 65, -r2, jnp.where(lane_c == 66, -r3, do))
            ).astype(bf16)
            q, k, v = (ref[h, rows, :].astype(f32) for ref in (qa, ka, va))
            drop = jnp.sum(jnp.where(lane_c == ml, k, 0.0), axis=1, keepdims=True) < -1.0
            own = jnp.sum(jnp.where(low | (lane_c > ml), q * k, 0.0), axis=1, keepdims=True)
            p_own = jnp.where(drop, jnp.exp(jnp.where(drop, own, 0.0)), 0.0)
            ds_own = p_own * (jnp.sum(jnp.where(low, do * v, 0.0), axis=1, keepdims=True) - row_dot)
            dqs[h, rows, :] = ds_own * k
            dka[h, rows, :] = ds_own * q
            dva[h, rows, :] = p_own * do
    per, perk = chunk // BQ, chunk // BK

    def qblock(b, _):
        off = pl.multiple_of(jnp.bitwise_xor(b // per, m) * chunk + (b % per) * BQ, BQ)
        rows = pl.ds(off, BQ)
        lo, hi = key_range(ends, b * BQ, b * BQ + BQ - 1)

        def kstep(kb, carry):
            koff = pl.multiple_of(jnp.bitwise_xor(kb // perk, m) * chunk + (kb % perk) * BK, BK)
            kr = pl.ds(koff, BK)
            out = []
            scores = [dot(ka[h, kr, :], qa[h, rows, :], NT) for h in range(heads)]
            dps = [dot(va[h, kr, :], doa[h, rows, :], NT) for h in range(heads)]
            for h in range(heads):
                p = jnp.exp(scores[h])
                ds = (p * dps[h]).astype(bf16)
                dva[h, kr, :] += dot(p.astype(bf16), doa[h, rows, :])
                dka[h, kr, :] += dot(ds, qa[h, rows, :])
                out.append(carry[h] + dot(ds, ka[h, kr, :], TN))
            return tuple(out)

        zeros = tuple(jnp.zeros((BQ, 128), f32) for _ in range(heads))
        fin = lax.fori_loop(lo // BK, (hi + BK - 1) // BK, kstep, zeros)
        for h in range(heads):
            dqs[h, rows, :] += fin[h]
        return 0

    lax.fori_loop(0, G // BQ, qblock, 0)
    sums[...] = jnp.zeros_like(sums)
    for c in range(G // chunk):
        rows = slice(c * chunk, (c + 1) * chunk)
        parts = [dqs[h, rows, :] * 0.125 for h in range(heads)]
        parts += [dka[h, rows, :] for h in range(heads)] + [dva[h, rows, :] for h in range(heads)]
        for i, tile in enumerate(pack_heads(parts, low)):
            tile = tile.astype(bf16)
            cols = slice(128 * i, 128 * i + tile.shape[1])
            out_ref[rows, cols] = tile
            sums[0:1, cols] += jnp.sum(tile.astype(f32), axis=0, keepdims=True)
    far_ref[...] = dot(out_ref[3 * chunk :, :], w_ref[...], NT).astype(bf16)
    far2_ref[...] = dot(out_ref[2 * chunk : 3 * chunk, :], w_ref[...], NT).astype(bf16)
    total = dot(x0[...], out_ref[:chunk, :], TN)
    for c, x in ((1, x1), (2, x2), (3, x3)):
        total = total + dot(x[...], out_ref[c * chunk : (c + 1) * chunk, :], TN)
    grad[...] = total
    wide = w_ref[...].astype(f32)
    gain = jnp.sum(wide * total, axis=1, keepdims=True)
    bias = jnp.sum(wide * sums[0:1, :], axis=1, keepdims=True)
    lane = lax.broadcasted_iota(jnp.int32, (wide.shape[0], 128), 1)
    both = jnp.where(lane == 0, gain, bias).T
    half = wide.shape[0] // 2
    vec = [both[j : j + 1, half * k : half * (k + 1)] for j in range(2) for k in range(2)]
    vec = jnp.concatenate(vec + [jnp.zeros((4, half), f32)], axis=0)
    vec_ref[...] = vec
    take_blocks(i_ref[0], grad, here_ref, other_ref, n)
    if n == 8:
        tops = top_rows(vec[0:4], wide.shape[1])
        rows = wide.shape[0] // n
        for z in range(n // 2):
            other_ref[z, rows:] = tops


def attend_backward(m, lengths, i, qs, ka, va, ofs, grads, xs, w, n, dep):
    heads, G, _ = ka.shape
    chunk, D = grads[0].shape[0], w.shape[0]
    W3 = 3 * heads * HD
    shapes = tuple(block_shapes(D, W3, n, 16))
    return pl.pallas_call(
        functools.partial(bwd_kernel, heads=heads, chunk=chunk, BQ=256, BK=256, nseq=lengths.shape[1], n=n),
        out_shape=(sds((G, W3), bf16),) + (sds((chunk, D), bf16),) * 2 + shapes + (sds((8, D // 2), f32),),
        in_specs=[SMEM_SPEC] * 3 + [VMEM_SPEC] * 15 + [ANY_SPEC],
        out_specs=[VMEM_SPEC] * 6,
        scratch_shapes=[pltpu.VMEM((heads, G, 128), bf16)] * 2
        + [pltpu.VMEM((heads, G, 128), f32)] * 3
        + [pltpu.VMEM((D, W3), f32), pltpu.VMEM((8, W3), f32)],
        compiler_params=AB_VMEM,
        cost_estimate=cost(40e9, 12e6, 6e6),
        name="attend_backward",
    )(m, lengths, i, *qs, ka, va, *ofs, *grads, *xs, w, dep)


def gelu_parts(u):
    z = jnp.abs(u) * 0.7071067811865476
    t = 1.0 / (1.0 + 0.3275911 * z)
    poly = t * (0.254829592 + t * (-0.284496736 + t * (1.421413741 + t * (-1.453152027 + t * 1.061405429))))
    e = jnp.exp(-z * z)
    tail = 0.5 * poly * e
    cdf = jnp.where(u >= 0, 1.0 - tail, tail)
    return u * cdf, cdf + u * (e * 0.3989422804014327)


def pick(i, half, first, second):
    return jnp.where(i < half, first[...], second[...])


def ffn_in_kernel(x0, x1, og0, og1, w_ref, v_ref, b_ref, g_ref, *refs, half):
    a_ref, gp_ref, e_ref, st_ref = refs[-4:]
    i = pl.program_id(0)
    a, gp = gelu_parts(dot(pick(i, half, x0, x1), w_ref[...]) + row(b_ref))
    e = dot(pick(i, half, og0, og1), v_ref[...])
    n = a.shape[1]
    mean = jnp.sum(a, axis=1, keepdims=True) * (1.0 / n)
    cent = a - mean
    m2 = jnp.sum(cent * cent, axis=1, keepdims=True)
    eg = e * row(g_ref)
    t1 = jnp.sum(eg, axis=1, keepdims=True)
    t2 = jnp.sum(eg * cent, axis=1, keepdims=True)
    a_ref[...] = a
    gp_ref[...] = gp.astype(bf16)
    e_ref[...] = e
    lane = lax.broadcasted_iota(jnp.int32, (a.shape[0], 128), 1)
    st = jnp.where(lane == 0, mean, jnp.where(lane == 1, m2, jnp.where(lane == 2, t1, t2)))
    st_ref[...] = st.T[:8]


def ffn_in(xs, ogs, fc, b, g, part, stats, rows=256):
    R, D = xs[0].shape
    F = b.shape[0]
    half = R // rows
    full = lambda i: (0, 0)
    row = lambda i: (i, 0)
    lower = pl.BlockSpec((rows, D), lambda i: (jnp.minimum(i, half - 1), 0))
    upper = pl.BlockSpec((rows, D), lambda i: (jnp.maximum(i - half, 0), 0))
    extra = () if stats is None else (stats,)
    return pl.pallas_call(
        functools.partial(ffn_in_kernel, half=half),
        grid=(2 * half,),
        in_specs=[
            lower,
            upper,
            lower,
            upper,
            pl.BlockSpec((D, F), full),
            pl.BlockSpec((D, F), lambda i: (0, 1)),
            whole(b),
            whole(g),
        ]
        + [ANY_SPEC] * len(extra),
        out_specs=[pl.BlockSpec((rows, F), row)] * 3 + [pl.BlockSpec((8, rows), lambda i: (0, 2 * half * part + i))],
        out_shape=[sds((2 * R, F), f32), sds((2 * R, F), bf16), sds((2 * R, F), f32), sds((8, 4 * R), f32)],
        input_output_aliases={8: 3} if extra else {},
        compiler_params=SMALL_VMEM,
        cost_estimate=cost(8 * R * D * F, 32 * R * F, 4 * R * F),
        name="ffn_in",
    )(*xs, *ogs, fc, fc, b, g, *extra)


def back_rows(a_ref, gp_ref, e_ref, stats, g_ref, b_ref, full_width):
    stats = [s[...] for s in stats]
    n = a_ref.shape[1]
    means = [s[0:1] for s in stats]
    mean = sum(means) / len(stats)
    m2 = sum(s[1:2] + n * (mu - mean) * (mu - mean) for s, mu in zip(stats, means))
    inv = lax.rsqrt(m2 / full_width + EPS)
    c1 = sum(s[2:3] for s in stats) / full_width
    c2 = inv * sum(s[3:4] + (mu - mean) * s[2:3] for s, mu in zip(stats, means)) / full_width
    sub = lax.broadcasted_iota(jnp.int32, (128, mean.shape[1]), 0)
    cols = jnp.where(sub == 0, mean, jnp.where(sub == 1, inv, jnp.where(sub == 2, c1, c2))).T
    mean, inv, c1, c2 = (cols[:, j : j + 1] for j in range(4))
    gain = row(g_ref)
    e = e_ref[...].astype(f32)
    u = (a_ref[...].astype(f32) - mean) * inv
    fl = (u * gain + row(b_ref)).astype(bf16)
    du = (gp_ref[...].astype(f32) * (inv * (e * gain - c1 - u * c2))).astype(bf16)
    return fl, e, u, du


def vector_sums(acc_ref, e, u, du):
    @pl.when(pl.program_id(0) == 0)
    def _():
        acc_ref[...] = jnp.zeros_like(acc_ref)

    acc_ref[0:1, :] += jnp.sum(e * u, axis=0, keepdims=True)
    acc_ref[1:2, :] += jnp.sum(e, axis=0, keepdims=True)
    acc_ref[2:3, :] += jnp.sum(du.astype(f32), axis=0, keepdims=True)


def by_half(i, half, values, firsts, seconds):
    @pl.when(i < half)
    def _():
        for v, out in zip(values, firsts):
            out[...] = v

    @pl.when(i >= half)
    def _():
        for v, out in zip(values, seconds):
            out[...] = v


def far_back_kernel(a_ref, gp_ref, e_ref, s0, s1, s2, s3, g_ref, b_ref, w_ref, fl0, fl1, du0, du1, dx0, dxa, dxb, acc_ref, *, full_width, half):
    i = pl.program_id(0)
    fl, e, u, du = back_rows(a_ref, gp_ref, e_ref, (s0, s1, s2, s3), g_ref, b_ref, full_width)
    dx = dot(du, w_ref[...], NT).astype(bf16)
    by_half(i, half, (fl, du), (fl0, du0), (fl1, du1))

    @pl.when(i < half)
    def _():
        dx0[...] = dx

    by_half(i, half + half // 2, (dx,), (dxa,), (dxb,))
    vector_sums(acc_ref, e, u, du)


def near_back_kernel(i_ref, a_ref, gp_ref, e_ref, s0, s1, s2, s3, g_ref, b_ref, w_ref, v_ref, *refs, full_width, n):
    (x0, x1, x2, x3, og0, og1, og2, og3, fl2, fl3, du2, du3, _), refs = refs[:13], refs[13:]
    dx0, dxa, dxb, acc_ref, y0, y1, y2, y3, here_ref, other_ref, token, grad = refs
    i = pl.program_id(0)
    fl, e, u, du = back_rows(a_ref, gp_ref, e_ref, (s0, s1, s2, s3), g_ref, b_ref, full_width)
    dx = dot(du, w_ref[...], NT).astype(bf16)

    @pl.when(i == 0)
    def _():
        dx0[...] = dx

    @pl.when(i == 1)
    def _():
        half = dxa.shape[0]
        dxa[...] = dx[:half]
        dxb[...] = dx[half:]

    vector_sums(acc_ref, e, u, du)
    fl_far = pick(i, 1, fl2, fl3)
    by_half(
        i,
        1,
        (dot(fl, v_ref[...], NT).astype(bf16), dot(fl_far, v_ref[...], NT).astype(bf16)),
        (y0, y2),
        (y1, y3),
    )
    F = fl.shape[1]
    first = dot(pick(i, 1, x0, x1), du, TN) + dot(pick(i, 1, x2, x3), pick(i, 1, du2, du3), TN)
    second = dot(pick(i, 1, og0, og1), fl, TN) + dot(pick(i, 1, og2, og3), fl_far, TN)

    @pl.when(i == 0)
    def _():
        grad[:, :F] = first
        grad[:, F:] = second

    @pl.when(i == 1)
    def _():
        grad[:, :F] += first
        grad[:, F:] += second
        token[...] = jnp.zeros_like(token)
        take_blocks(i_ref[0], grad, here_ref, other_ref, n)


def take_blocks(i, grad, here_ref, other_ref, n):
    if n == 8:
        me = i % 2
        rows = grad.shape[0] // n
        for z in range(n // 2):
            at = pl.multiple_of((2 * z + me) * rows, rows)
            here_ref[z] = grad[pl.ds(at, rows), :]
            at = pl.multiple_of((2 * z + 1 - me) * rows, rows)
            other_ref[z, :rows] = grad[pl.ds(at, rows), :].astype(bf16)
    else:
        here_ref[...] = grad[...]
        other_ref[...] = jnp.zeros_like(other_ref)


def block_shapes(D, cols, n, extra=0):
    if n == 8:
        return [sds((n // 2, D // n, cols), f32), sds((n // 2, D // n + extra, cols), bf16)]
    return [sds((D, cols), f32), sds((16, 128), bf16)]


def ffn_back(parts, part, stats, g, b, fc, R, full_width, rows=256):
    a, gp, e = parts
    F, D = a.shape[1], fc.shape[0]
    half = R // rows
    line = lambda i: (i, 0)
    place = lambda k: lambda i: (0, ((2 * part + i // half) ^ k) * half + i % half)
    lower = lambda i: (jnp.minimum(i, half - 1), 0)
    upper = lambda i: (jnp.maximum(i - half, 0), 0)
    pair = lambda n: [pl.BlockSpec((rows, n), lower), pl.BlockSpec((rows, n), upper)]
    dx_specs = [
        pl.BlockSpec((rows, D), lower),
        pl.BlockSpec((rows, D), lambda i: (jnp.clip(i - half, 0, half // 2 - 1), 0)),
        pl.BlockSpec((rows, D), lambda i: (jnp.maximum(i - half - half // 2, 0), 0)),
        pl.BlockSpec((8, F), lambda i: (0, 0)),
    ]
    dx_shapes = [sds((R, D), bf16)] + [sds((R // 2, D), bf16)] * 2 + [sds((8, F), f32)]
    in_specs = (
        [pl.BlockSpec((rows, F), line)] * 3
        + [pl.BlockSpec((8, rows), place(k)) for k in range(4)]
        + [whole(g), whole(b), pl.BlockSpec((D, F), lambda i: (0, 0))]
    )
    operands = (a, gp, e, *stats, g, b, fc)
    return half, pair, in_specs, operands, dx_specs, dx_shapes


def far_back(parts, stats, g, b, fc, R, full_width):
    half, pair, in_specs, operands, dx_specs, dx_shapes = ffn_back(parts, 1, stats, g, b, fc, R, full_width)
    F = parts[0].shape[1]
    return pl.pallas_call(
        functools.partial(far_back_kernel, full_width=full_width, half=half),
        grid=(2 * half,),
        in_specs=in_specs,
        out_specs=pair(F) * 2 + dx_specs,
        out_shape=[sds((R, F), bf16)] * 4 + dx_shapes,
        compiler_params=SMALL_VMEM,
        cost_estimate=cost(1, 1),
        name="far_back",
    )(*operands)


def near_back(i, parts, stats, g, b, fc, R, full_width, hl, og, fl, du, n, dep):
    _, _, in_specs, operands, _, dx_shapes = ffn_back(parts, 0, stats, g, b, fc, R, full_width, R)
    F, D = parts[0].shape[1], fc.shape[0]
    blocks = block_shapes(D, 2 * F, n)
    shapes = dx_shapes + [sds((R, D), bf16)] * 4 + blocks + [sds((8, 128), f32)]
    return pl.pallas_call(
        functools.partial(near_back_kernel, full_width=full_width, n=n),
        grid=(2,),
        in_specs=[SMEM_SPEC]
        + in_specs
        + [pl.BlockSpec((D, F), lambda i: (0, 1))]
        + [whole(x) for x in hl + og + fl + du]
        + [ANY_SPEC],
        out_specs=[whole(x) for x in shapes],
        out_shape=shapes,
        scratch_shapes=[pltpu.VMEM((D, 2 * F), f32)],
        compiler_params=MID_VMEM,
        cost_estimate=cost(1, 1),
        name="near_back",
    )(i, *operands, fc, *hl, *og, *fl, *du, dep)


def combine_kernel(z_ref, here_ref, got_ref, *refs, extra):
    z = z_ref[0] // 2
    nz, rows, cols = here_ref.shape
    own_ref = refs[-4]
    if extra:
        vec_ref, vec_out = refs[0], refs[-5]
        vectors = vec_ref[...]
        for j in range(2):
            for i in range(2):
                parts = [got_ref[0, rows + 4 * t + 2 * j + i : rows + 4 * t + 2 * j + i + 1, :extra] for t in range(3)]
                add_to = sum(p.astype(f32) for p in parts)
                vec_out[2 * j + i : 2 * j + i + 1, :] = vectors[2 * j + i : 2 * j + i + 1, :] + add_to
        vec_out[4:, :] = jnp.zeros((4, extra), f32)
        tops = top_rows(vec_out[0:4, :], cols)
    for k, out in enumerate((own_ref,) + tuple(refs[-3:])):
        at = (z + k) % nz
        block = here_ref[pl.ds(at, 1)][0] + got_ref[pl.ds(at, 1)][0][:rows].astype(f32)
        if k:
            out[:rows, :] = block.astype(bf16)
            if extra:
                out[rows:, :] = tops
        else:
            out[...] = block


def top_rows(vectors, cols):
    half = vectors.shape[1]
    tops = jnp.concatenate(list(split3(vectors)) + [jnp.zeros((4, half), f32)], axis=0)
    return jnp.concatenate([tops, jnp.zeros((16, cols - half), f32)], axis=1).astype(bf16)


def combine(i, here, got, vec=None, deps=()):
    nz, rows, cols = here.shape
    more = 0 if vec is None else 16
    return pl.pallas_call(
        functools.partial(combine_kernel, extra=0 if vec is None else vec.shape[1]),
        out_shape=([] if vec is None else [sds(vec.shape, f32)])
        + [sds((rows, cols), f32)]
        + [sds((rows + more, cols), bf16)] * 3,
        in_specs=[SMEM_SPEC] + [VMEM_SPEC] * (2 if vec is None else 3) + [ANY_SPEC] * len(deps),
        out_specs=[VMEM_SPEC] * (4 if vec is None else 5),
        compiler_params=SMALL_VMEM,
        cost_estimate=cost(8 * rows * cols, 40 * rows * cols),
        name="combine",
    )(i, here, got, *([] if vec is None else [vec]), *deps)


def gate_kernel(*refs):
    pass


def gate(xs, *others):
    n = len(xs)
    return pl.pallas_call(
        gate_kernel,
        out_shape=[sds(x.shape, x.dtype) for x in xs],
        in_specs=[ANY_SPEC] * (n + len(others)),
        out_specs=[ANY_SPEC] * n,
        input_output_aliases={i: i for i in range(n)},
        compiler_params=SMALL_VMEM,
        cost_estimate=cost(1, 1),
        name="gate",
    )(*xs, *others)


def put_kernel(t0, t1, v_ref, q1, q2, q3, out_ref, token, *, n):
    W = t0.shape[0] // 2
    both = (t0[...].astype(f32) + t1[...].astype(f32)).T
    near, far = both[:, :W], both[:, W:]
    D = near.shape[0]
    vectors = v_ref[...]
    rows = vectors.shape[0]
    for q in (q1, q2, q3):
        vectors = vectors + q[q.shape[0] - rows :, :128].astype(f32)
    token[...] = vectors
    vectors = jnp.concatenate([vectors] * n if rows * n == D else [jnp.zeros((D, 128), f32)], axis=0)
    out_ref[:, :256] = jnp.concatenate([near, vectors[:, :64]], axis=1).astype(bf16)
    out_ref[:, 256:] = jnp.concatenate([far, vectors[:, 64:]], axis=1).astype(bf16)


def put(ts, v, qs, n):
    D = ts[0].shape[1]
    return pl.pallas_call(
        functools.partial(put_kernel, n=n),
        out_shape=[sds((D, 512), bf16), sds(v.shape, f32)],
        in_specs=[VMEM_SPEC] * 6,
        out_specs=[VMEM_SPEC] * 2,
        compiler_params=SMALL_VMEM,
        cost_estimate=cost(1, 1),
        name="put",
    )(*ts, v, *qs)


def unpack_kernel(x_ref, got_ref, out_ref, *v_refs):
    W = out_ref.shape[0]
    near = x_ref[:, :256].astype(f32)
    out_ref[...] = (near + got_ref[...].astype(f32)).T[:W]
    far = x_ref[:, 256:].astype(f32)
    vectors = jnp.concatenate([near[:, W:], far[:, W:]], axis=1)
    at = 0
    for v in v_refs:
        v[...] = vectors[at : at + v.shape[0]]
        at += v.shape[0]


def unpack(rows, got, W, sizes):
    n = rows.shape[0]
    shapes = [sds((W, n), f32)] + [sds((k // 128, 128), f32) for k in sizes]
    return pl.pallas_call(
        unpack_kernel,
        out_shape=shapes,
        in_specs=[VMEM_SPEC] * 2,
        out_specs=[VMEM_SPEC] * len(shapes),
        compiler_params=SMALL_VMEM,
        cost_estimate=cost(1, 1),
        name="unpack",
    )(rows, got)


def fc_sums_kernel(own_ref, s1, s2, s3, fc1_ref, fc2_ref):
    F = fc1_ref.shape[1]
    total = own_ref[...] + s1[...].astype(f32) + s2[...].astype(f32) + s3[...].astype(f32)
    fc1_ref[...] = total[:, :F]
    fc2_ref[...] = total[:, F:]


def fc_sums(own, got):
    rows, cols = own.shape
    return pl.pallas_call(
        fc_sums_kernel,
        out_shape=[sds((rows, cols // 2), f32)] * 2,
        in_specs=[VMEM_SPEC] * 4,
        out_specs=[VMEM_SPEC] * 2,
        compiler_params=SMALL_VMEM,
        cost_estimate=cost(1, 1),
        name="fc_sums",
    )(own, *got)


def qkv_sums_kernel(own_ref, v_ref, s1, s2, s3, *refs):
    out_ref, v_out = refs[-2:]
    rows = own_ref.shape[0]
    W = out_ref.shape[2]
    half = v_ref.shape[1]
    got = s1[...].astype(f32) + s2[...].astype(f32) + s3[...].astype(f32)
    total = own_ref[...] + got[:rows]
    for c in range(3):
        out_ref[c] = total[:, c * W : (c + 1) * W]
    tops = got[rows : rows + 8, :half]
    v_out[0:4, :] = v_ref[0:4, :] + tops[0:4] + tops[4:8] + got[rows + 8 : rows + 12, :half]
    v_out[4:8, :] = jnp.zeros((4, half), f32)


def qkv_sums(own, vec, got, W, deps):
    rows = own.shape[0]
    return pl.pallas_call(
        qkv_sums_kernel,
        out_shape=[sds((3, rows, W), f32), sds(vec.shape, f32)],
        in_specs=[VMEM_SPEC] * 5 + [ANY_SPEC] * len(deps),
        out_specs=[VMEM_SPEC] * 2,
        compiler_params=SMALL_VMEM,
        cost_estimate=cost(1, 1),
        name="qkv_sums",
    )(own, vec, *got, *deps)


def finish_kernel(v0, v1, v2, v3, b_ref, g_ref, gain_ref, bias_ref):
    v = v0[...] + v1[...] + v2[...] + v3[...]
    gain = jnp.concatenate([v[0:1], v[1:2]], axis=1)
    bias = jnp.concatenate([v[2:3], v[3:4]], axis=1)
    gain = (gain - row(b_ref) * bias) / row(g_ref)
    for t in range(gain_ref.shape[0]):
        cols = slice(128 * t, 128 * (t + 1))
        bias_ref[t : t + 1, :] = bias[:, cols]
        gain_ref[t : t + 1, :] = gain[:, cols]


def finish(vs, b, g):
    D = b.shape[0]
    return pl.pallas_call(
        finish_kernel,
        out_shape=[sds((D // 128, 128), f32)] * 2,
        in_specs=[VMEM_SPEC] * 6,
        out_specs=[VMEM_SPEC] * 2,
        compiler_params=SMALL_VMEM,
        cost_estimate=cost(1, 1),
        name="finish",
    )(*vs, b, g)


def norm_parts(values):
    mean = jnp.mean(values, axis=-1, keepdims=True)
    cent = values - mean
    inv = lax.rsqrt(jnp.mean(cent * cent, axis=-1, keepdims=True) + EPS)
    return cent * inv, inv


def pieces_norm(pieces, width):
    mean = sum(jnp.sum(p, axis=1, keepdims=True) for p in pieces) * (1.0 / width)
    cents = [p - mean for p in pieces]
    var = sum(jnp.sum(c * c, axis=1, keepdims=True) for c in cents) * (1.0 / width)
    inv = lax.rsqrt(var + EPS)
    return [c * inv for c in cents], inv


def row(ref):
    return ref[...].reshape(1, ref.shape[0])


def gain_rows(ow_ref, D):
    rows = ow_ref[D : D + 16, :].astype(f32)
    return rows[0:1] + rows[1:2] + rows[2:3], rows[3:4] + rows[4:5] + rows[5:6]


def in_norm_kernel(x_ref, g_ref, b_ref, out_ref):
    unit, _ = norm_parts(x_ref[...].astype(f32))
    out_ref[...] = (unit * row(g_ref) + row(b_ref)).astype(bf16)


def mix_kernel(p0, p1, p2, p3, w0, w1, w2, w3, x_ref, g_ref, b_ref, h_ref, hl_ref):
    D = x_ref.shape[1]
    units, _ = pieces_norm([p[...].astype(f32) for p in (p0, p1, p2, p3)], D)
    h = x_ref[...].astype(f32)
    for unit, w in zip(units, (w0, w1, w2, w3)):
        gain, bias = gain_rows(w, D)
        h = h + dot((unit * gain + bias).astype(bf16), w[:D, :], NT)
    h_ref[...] = h
    unit, _ = norm_parts(h)
    hl_ref[...] = (unit * row(g_ref) + row(b_ref)).astype(bf16)


def mix(pieces, ows, x, g, b, rows=256):
    R, D = x.shape
    W = pieces[0].shape[1]
    full = lambda i: (0, 0)
    row = lambda i: (i, 0)
    return pl.pallas_call(
        mix_kernel,
        grid=(R // rows,),
        in_specs=[pl.BlockSpec((rows, W), row)] * 4
        + [pl.BlockSpec((D + 16, W), full)] * 4
        + [pl.BlockSpec((rows, D), row), whole(g), whole(b)],
        out_specs=[pl.BlockSpec((rows, D), row)] * 2,
        out_shape=[sds((R, D), f32), sds((R, D), bf16)],
        compiler_params=SMALL_VMEM,
        cost_estimate=cost(1, 1),
        name="mix",
    )(*pieces, *ows, x, g, b)


def mix_back_kernel(m_ref, da_ref, ca_ref, cb_ref, db_ref, h_ref, og_ref, p0, p1, p2, p3, w0, w1, w2, w3, g_ref, hn_ref, hf_ref, dep0, dep1, dh_ref, q0, q1, q2, q3, on_ref, of_ref, v_ref, acc, fs_ref, ms_ref, qs_ref):
    D = h_ref.shape[1]
    m = m_ref[0]
    i = pl.program_id(0)

    @pl.when(i == 0)
    def _():
        acc[...] = jnp.zeros_like(acc)
        fs_ref[...] = jnp.zeros_like(fs_ref)
        ms_ref[...] = jnp.zeros_like(ms_ref)

    beside = pick(i, pl.num_programs(0) // 2, ca_ref, cb_ref)
    dhl = da_ref[...].astype(f32) + beside.astype(f32) + db_ref[...].astype(f32)
    unit, inv = norm_parts(h_ref[...])
    scaled = dhl * row(g_ref)
    first = jnp.mean(scaled, axis=1, keepdims=True)
    second = jnp.mean(scaled * unit, axis=1, keepdims=True)
    dh = og_ref[...].astype(f32) + inv * (scaled - first - unit * second)
    dh_ref[...] = dh
    fs_ref[0:1, :] += jnp.sum(dhl * unit, axis=0, keepdims=True)
    fs_ref[1:2, :] += jnp.sum(dhl, axis=0, keepdims=True)
    dhr = dh.astype(bf16)
    units, inv = pieces_norm([p[...].astype(f32) for p in (p0, p1, p2, p3)], D)
    scaleds = []
    for k, (unit, w) in enumerate(zip(units, (w0, w1, w2, w3))):
        gain, bias = gain_rows(w, D)
        dol = dot(dhr, w[:D, :])
        acc[k] += dot((unit * gain + bias).astype(bf16), dhr, TN)
        at = jnp.bitwise_xor(m, k)
        ms_ref[pl.ds(at, 1), :] += jnp.sum(dol * unit, axis=0, keepdims=True)
        ms_ref[pl.ds(4 + at, 1), :] += jnp.sum(dol, axis=0, keepdims=True)
        scaleds.append(dol * gain)
    first = sum(jnp.sum(s, axis=1, keepdims=True) for s in scaleds) * (1.0 / D)
    second = sum(jnp.sum(s * u, axis=1, keepdims=True) for s, u in zip(scaleds, units)) * (1.0 / D)
    R = p0.shape[0]
    at = pl.ds(pl.multiple_of(i * R, R), R)
    for k, (s, u) in enumerate(zip(scaleds, units)):
        q = (inv * (s - first - u * second)).astype(bf16)
        if k:
            qs_ref[k - 1, at, :] = q
        else:
            q0[...] = q

    @pl.when(i == pl.num_programs(0) - 1)
    def _():
        W = p0.shape[1]
        for j in range(2):
            on_ref[j * W : (j + 1) * W, :] = acc[2 * j].astype(bf16)
            of_ref[j * W : (j + 1) * W, :] = acc[2 * j + 1].astype(bf16)
        hidden = hn_ref[...] + hf_ref[...]
        v_ref[...] = jnp.zeros_like(v_ref)
        tiles = D // 128
        mixed = [jnp.concatenate([ms_ref[4 * j + k : 4 * j + k + 1, :] for k in range(4)], axis=1) for j in range(2)]
        for t in range(tiles):
            cols = slice(128 * t, 128 * (t + 1))
            for j in range(3):
                v_ref[pl.ds(4 * tiles * j + tiles * m + t, 1), :] = hidden[j : j + 1, cols]
            for j in range(2):
                at = 12 * tiles + tiles * j + t
                v_ref[at : at + 1, :] = fs_ref[j : j + 1, cols]
                at += 2 * tiles
                v_ref[at : at + 1, :] = mixed[j][:, cols]
        rows = qs_ref.shape[1]
        for k, q in enumerate((q1, q2, q3)):
            q[:rows, :] = qs_ref[k]
            q[rows:, :128] = v_ref[...].astype(bf16)
            q[rows:, 128:] = jnp.zeros((q.shape[0] - rows, q.shape[1] - 128), bf16)


def mix_back(m, da, dc, db, h, og, pieces, ows, g, hidden, deps, rows=256):
    R, D = h.shape
    W = pieces[0].shape[1]
    full = lambda i: (0, 0)
    row = lambda i: (i, 0)
    wide = pl.BlockSpec((rows, D), row)
    piece = pl.BlockSpec((rows, W), row)
    halves = R // rows // 2
    extra = 16 * D // 128
    return pl.pallas_call(
        mix_back_kernel,
        grid=(R // rows,),
        in_specs=[
            SMEM_SPEC,
            wide,
            pl.BlockSpec((rows, D), lambda i: (jnp.minimum(i, halves - 1), 0)),
            pl.BlockSpec((rows, D), lambda i: (jnp.maximum(i - halves, 0), 0)),
        ]
        + [wide] * 3
        + [piece] * 4
        + [pl.BlockSpec((D + 16, W), full)] * 4
        + [whole(g), whole(hidden[0]), whole(hidden[1])]
        + [ANY_SPEC] * 2,
        out_specs=[wide, piece]
        + [pl.BlockSpec((R + extra, W), full)] * 3
        + [pl.BlockSpec((2 * W, D), full)] * 2
        + [pl.BlockSpec((extra, 128), full)],
        out_shape=[sds((R, D), f32)]
        + [sds((R, W), bf16)]
        + [sds((R + extra, W), bf16)] * 3
        + [sds((2 * W, D), bf16)] * 2
        + [sds((extra, 128), f32)],
        scratch_shapes=[
            pltpu.VMEM((4, W, D), f32),
            pltpu.VMEM((8, D), f32),
            pltpu.VMEM((8, W), f32),
            pltpu.VMEM((3, R, W), bf16),
        ],
        compiler_params=SMALL_VMEM,
        cost_estimate=cost(2e10, 1),
        name="mix_back",
    )(m, da, *dc, db, h, og, *pieces, *ows, g, *hidden, *deps)


def last_kernel(da_ref, ca_ref, cb_ref, db_ref, x_ref, dh_ref, g_ref, out_ref):
    unit, inv = norm_parts(x_ref[...].astype(f32))
    beside = pick(pl.program_id(0), pl.num_programs(0) // 2, ca_ref, cb_ref)
    scaled = (da_ref[...].astype(f32) + beside.astype(f32) + db_ref[...].astype(f32)) * row(g_ref)
    first = jnp.mean(scaled, axis=1, keepdims=True)
    second = jnp.mean(scaled * unit, axis=1, keepdims=True)
    out_ref[...] = dh_ref[...] + inv * (scaled - first - unit * second)


def rows_call(kernel, name, arrays, vectors, out_type, rows=256):
    R, D = arrays[0].shape
    n = R // rows
    wide = pl.BlockSpec((rows, D), lambda i: (i, 0))
    lower = pl.BlockSpec((rows, D), lambda i: (jnp.minimum(i, n // 2 - 1), 0))
    upper = pl.BlockSpec((rows, D), lambda i: (jnp.maximum(i - n // 2, 0), 0))
    specs, operands = [], []
    for x in arrays:
        specs += [lower, upper] if isinstance(x, list) else [wide]
        operands += x if isinstance(x, list) else [x]
    return pl.pallas_call(
        kernel,
        grid=(n,),
        in_specs=specs + [whole(v) for v in vectors],
        out_specs=wide,
        out_shape=sds((R, D), out_type),
        compiler_params=SMALL_VMEM,
        cost_estimate=cost(20 * R * D, 16 * R * D),
        name=name,
    )(*operands, *vectors)


def project_two_kernel(x_ref, w_ref, dep, out0, outa, outb, *, half):
    y = dot(x_ref[...], w_ref[...], NT).astype(bf16)
    i = pl.program_id(0)

    @pl.when(i < half // 2)
    def _():
        outa[...] = y

    @pl.when((i >= half // 2) & (i < half))
    def _():
        outb[...] = y

    @pl.when(i >= half)
    def _():
        out0[...] = y


def project_two(x, w, R, dep, rows=256):
    D = w.shape[0]
    half = R // rows
    return pl.pallas_call(
        functools.partial(project_two_kernel, half=half),
        grid=(2 * half,),
        in_specs=[pl.BlockSpec((rows, x.shape[1]), lambda i: ((i + half) % (2 * half), 0)), whole(w), ANY_SPEC],
        out_specs=[
            pl.BlockSpec((rows, D), lambda i: (jnp.maximum(i - half, 0), 0)),
            pl.BlockSpec((rows, D), lambda i: (jnp.minimum(i, half // 2 - 1), 0)),
            pl.BlockSpec((rows, D), lambda i: (jnp.clip(i - half // 2, 0, half // 2 - 1), 0)),
        ],
        out_shape=[sds((R, D), bf16)] + [sds((R // 2, D), bf16)] * 2,
        compiler_params=SMALL_VMEM,
        cost_estimate=cost(1, 1),
        name="project_two",
    )(x, w, dep)


def swap(x, axis, k):
    n = lax.axis_size(axis)
    return lax.ppermute(x, axis, [(i, i ^ k) for i in range(n)])


def shift(x, axis, k):
    n = lax.axis_size(axis)
    return lax.ppermute(x, axis, [(i, (i + k) % n) for i in range(n)])


def place_kernel(i_ref, *refs, cols, hops):
    pieces, (gains, og_ref, x2, w_ref, ow_ref, og_out, x2_out) = refs[:hops], refs[hops:]
    rows, D = pieces[0].shape[0], w_ref.shape[0]
    for j, piece in enumerate(pieces):
        owner = jnp.bitwise_xor((i_ref[0] + hops - 2 * (j // 2)) % hops, j % 2)
        at = pl.ds(pl.multiple_of(owner * rows, rows), rows)
        w_ref[at, :] = piece[:, :cols]
        ow_ref[at, :] = piece[:, cols:]
    ow_ref[D : D + 16, :] = gains[...]
    og_out[...] = og_ref[...]


def gather_first(w, gains, cols, og, x2):
    n = lax.axis_size("dp")
    if n != 8:
        full = lax.all_gather(w, "dp", axis=0, tiled=True)
        return full[:, :cols], jnp.concatenate([full[:, cols:], gains], axis=0), og, x2
    pieces, here = [], w
    for hop in range(4):
        pieces += [here, swap(here, "dp", 1)]
        if hop < 3:
            here = shift(here, "dp", 2)
    D = n * w.shape[0]
    i = lax.axis_index("dp").astype(jnp.int32).reshape(1)
    return pl.pallas_call(
        functools.partial(place_kernel, cols=cols, hops=n),
        out_shape=(
            sds((D, cols), bf16),
            sds((D + 16, w.shape[1] - cols), bf16),
            sds(og.shape, og.dtype),
            sds(x2.shape, x2.dtype),
        ),
        in_specs=[SMEM_SPEC] + [VMEM_SPEC] * (n + 2) + [ANY_SPEC],
        out_specs=[VMEM_SPEC] * 3 + [ANY_SPEC],
        input_output_aliases={n + 3: 3},
        compiler_params=SMALL_VMEM,
        cost_estimate=cost(0, 4 * D * w.shape[1]),
        name="place",
    )(i, *pieces, gains, og, x2)


def sum_all(x):
    for axis in ("mp", "dp"):
        k, n = 1, lax.axis_size(axis)
        while k < n:
            x = x + swap(x, axis, k)
            k *= 2
    return x


def per_device(
    layer_input,
    lengths,
    key_mask,
    input_gain,
    input_bias,
    qkv_weight,
    mixed_gain,
    mixed_bias,
    out_weight,
    ffn_gain,
    ffn_bias,
    fc1_weight,
    fc1_bias,
    hidden_gain,
    hidden_bias,
    fc2_weight,
    out_grad,
):
    R, D = layer_input.shape
    W = out_weight.shape[0]
    F = fc1_bias.shape[0]
    mp = lax.axis_size("mp")
    heads = W // HD
    m = lax.axis_index("mp").astype(jnp.int32)
    m1 = m.reshape(1)
    shard = qkv_weight.shape[0]
    n_dp = lax.axis_size("dp")
    dp1 = lax.axis_index("dp").astype(jnp.int32).reshape(1)

    x0 = rows_call(in_norm_kernel, "in_norm", [layer_input], [input_gain, input_bias], bf16)
    x2 = swap(x0, "mp", 2)
    x1 = swap(x0, "mp", 1)
    gains = [t.astype(bf16) for t in split3(mixed_gain) + split3(mixed_bias)]
    gains = jnp.concatenate([jnp.stack(gains), jnp.zeros((10, W), bf16)], axis=0)
    first_w = jnp.concatenate([qkv_weight.reshape(shard, 3 * W), out_weight.T], axis=1)
    qkv_full, ow, og0, x2 = gather_first(first_w, gains, 3 * W, out_grad, x2)
    fc = lax.all_gather(jnp.concatenate([fc1_weight, fc2_weight.T], axis=1), "dp", axis=0, tiled=True)
    ow2 = swap(ow, "mp", 2)
    ow1 = swap(ow, "mp", 1)
    og2 = swap(og0, "mp", 2)
    og1 = swap(og0, "mp", 1)
    xl = [x0, x1, x2, swap(x2, "mp", 1)]

    o2, o3, of_far, q_far, q_near, ka, va = attend_far(m1, lengths, key_mask, xl, qkv_full, heads)
    o0, o1, of_near, q_near = attend_near(m1, lengths, q_near, ka, va)
    pieces = [o0] + [swap(o, "mp", k) for k, o in ((1, o1), (2, o2), (3, o3))]
    ow2, og2 = tie([ow2, og2], o0, *pieces[2:])
    ows = [ow, ow1, ow2, swap(ow2, "mp", 1)]
    og = [og0, og1, og2, swap(og2, "mp", 1)]
    h, hl0 = mix(pieces, ows, layer_input, ffn_gain, ffn_bias)
    hl2 = swap(hl0, "mp", 2)
    hl1 = swap(hl0, "mp", 1)
    near = ffn_in([hl0, hl1], og[:2], fc, fc1_bias, hidden_gain, 0, None)
    hl2 = tie([hl2], near[0])[0]
    hl = [hl0, hl1, hl2, swap(hl2, "mp", 1)]
    far = ffn_in(hl[2:], og[2:], fc, fc1_bias, hidden_gain, 1, near[3])
    stats = [far[3]] + [swap(far[3], "mp", k) for k in (1, 2, 3)]
    norm_in = (stats, hidden_gain, hidden_bias, fc, R, mp * F)
    fl2, fl3, du2, du3, dx2, dx3a, dx3b, s_far = far_back(far[:3], *norm_in)
    dx3 = jnp.concatenate([swap(dx3a, "mp", 1), swap(dx3b, "mp", 1)], axis=0)
    dx2 = (dx2.astype(f32) + dx3.astype(f32)).astype(bf16)
    arrived = swap(dx2, "mp", 2)
    dx0, dx1a, dx1b, s_near, y0, y1, y2, y3, fc_here, fc_other, token = near_back(
        dp1, near[:3], *norm_in, hl, og, [fl2, fl3], [du2, du3], n_dp, dx2
    )
    beside = [swap(dx1a, "mp", 1), swap(dx1b, "mp", 1)]
    dh, q0, q1, q2, q3, t0, t1, vectors = mix_back(
        m1, dx0, beside, arrived, h, out_grad, pieces, ows, ffn_gain, [s_near, s_far], [token, token]
    )
    grads = [q0] + [swap(q, "mp", k) for k, q in ((1, q1), (2, q2), (3, q3))]
    ts = [t0, swap(t1, "mp", 1)]
    w_rows, vectors = put(ts, vectors, grads[1:], n_dp)
    w_rows = lax.psum_scatter(w_rows, "dp", scatter_dimension=0, tiled=True)
    y2 = add([y2, swap(y3, "mp", 1)], vectors)
    if n_dp == 8:
        fc_own, *sent = combine(dp1, fc_here, swap(fc_other, "dp", 1), deps=[y2])
        fc_sent = [shift(b, "dp", 2 * k) for k, b in ((1, sent[0]), (2, sent[1]), (3, sent[2]))]
    y2 = swap(y2, "mp", 2)

    dqkv, dx2, dx3, here, other, late = attend_backward(
        m1, lengths, dp1, [q_near, q_far], ka, va, [of_near, of_far], grads, xl, qkv_full, n_dp, vectors
    )
    if n_dp == 8:
        dx3, other = gate([dx3, other], y2, *fc_sent)
    dx2 = add([dx2, swap(dx3, "mp", 1)])
    arrived = swap(dx2, "mp", 2)
    dx0, dx1a, dx1b = project_two(dqkv, qkv_full, R, dx2)
    beside = [swap(dx1a, "mp", 1), swap(dx1b, "mp", 1)]
    layer_output = (h + (y0.astype(f32) + swap(y1, "mp", 1).astype(f32) + y2.astype(f32))).astype(bf16)
    if n_dp == 8:
        fc1_grad, fc2_grad = fc_sums(fc_own, fc_sent)
        late, own, *sent = combine(dp1, here, swap(other, "dp", 1), late, [fc1_grad, dx0, layer_output])
        sent = [shift(b, "dp", 2 * k) for k, b in ((1, sent[0]), (2, sent[1]), (3, sent[2]))]
    input_grad = rows_call(last_kernel, "last", [dx0, beside, arrived, layer_input, dh], [input_gain], f32)

    far_rows = swap(w_rows[:, 256:], "mp", 2)
    sizes = [mp * F] * 3 + [D] * 4
    if n_dp == 8:
        qkv_grad, late = qkv_sums(own, late, sent, W, [input_grad])
        qkv_grad = jnp.transpose(qkv_grad, (1, 0, 2))
        gain_grad, bias_grad = finish([late] + [swap(late, "mp", k) for k in (1, 2, 3)], input_bias, input_gain)
        gain_grad, bias_grad = gain_grad.reshape(D), bias_grad.reshape(D)
        out_grads, *parts = unpack(w_rows, far_rows, W, sizes)
        parts = [v.reshape(-1) for v in parts]
    else:
        qkv_grad = lax.psum_scatter(here, "dp", scatter_dimension=0, tiled=True).reshape(shard, 3, W)
        late = sum_all(late)[:4].reshape(2, D)
        bias_grad = late[1]
        gain_grad = (late[0] - input_bias * bias_grad) / input_gain
        fc_rows = lax.psum_scatter(fc_here, "dp", scatter_dimension=0, tiled=True)
        fc1_grad, fc2_grad = fc_rows[:, :F], fc_rows[:, F:]
        out_grads = (w_rows[:, :W].astype(f32) + far_rows[:, :W].astype(f32)).T
        k = 1
        while k < n_dp:
            vectors = vectors + swap(vectors, "dp", k)
            k *= 2
        flat = vectors.reshape(-1)
        parts, at = [], 0
        for size in sizes:
            parts.append(flat[at : at + size])
            at += size
    return (
        layer_output,
        input_grad,
        gain_grad,
        bias_grad,
        qkv_grad,
        parts[5],
        parts[6],
        out_grads,
        parts[3],
        parts[4],
        fc1_grad,
        parts[2],
        parts[0],
        parts[1],
        fc2_grad.T,
    )


def solution(mesh):
    return jax.shard_map(
        per_device,
        mesh=mesh,
        in_specs=(
            P(("dp", "mp"), None),
            P("dp", None),
            P("dp"),
            P(),
            P(),
            P("dp", None, "mp"),
            P("mp"),
            P("mp"),
            P("mp", "dp"),
            P(),
            P(),
            P("dp", "mp"),
            P("mp"),
            P("mp"),
            P("mp"),
            P("mp", "dp"),
            P(("dp", "mp"), None),
        ),
        out_specs=(
            P(("dp", "mp"), None),
            P(("dp", "mp"), None),
            P(),
            P(),
            P("dp", None, "mp"),
            P(),
            P(),
            P("mp", "dp"),
            P(),
            P(),
            P("dp", "mp"),
            P(),
            P(),
            P(),
            P("mp", "dp"),
        ),
        check_vma=False,
    )
```
